32 devices in a mesh: seq: 8 (over z, y), head: 4 (over x, core).
Axes of the slice: x: 2, y: 2, z: 4, core: 2. Of those that a mesh axis runs over, the one named last changes fastest.
Arguments:
- query_raw: bfloat16 [4096, 4096], P('seq', 'head'), may hold values from -600 to 600
- key_before_norm: bfloat16 [4096, 2048], P('seq', 'head'), may hold values from -600 to 600
- value_input: bfloat16 [4096, 2048], P('seq', 'head'), may hold values from -6 to 6
- out_cotangent: bfloat16 [4096, 4096], P('seq', 'head'), may hold values from -6 to 6
- query_gain: float32 [128], replicated, may hold values from 0.5 to 7
- key_norm_gain: float32 [128], replicated, may hold values from 0.5 to 7
- doc_starts: int32 [4, 8], replicated, may hold values from 0 to 1023, as said below
- windows: int32 [4], replicated, may hold values from 513 to 1024, as said below
Outputs:
- query_gradient: bfloat16 [4096, 4096], P('seq', 'head')
- key_gradient: bfloat16 [4096, 2048], P('seq', 'head')
- value_gradient: bfloat16 [4096, 2048], P('seq', 'head')
- query_norm_gain_gradient: float32 [128], replicated
- key_norm_gain_gradient: float32 [128], replicated
The draws below stay inside these ranges and needn't reach their ends.
Inputs may be any that keep to these rules, and one draw needn't show every extreme that they name: `doc_starts`: each row begins with 0 and rises strictly; no document starts at position 512. `windows`: some sequence has a window of exactly 1024.
All inputs are finite; a program needn't handle non-finite values.
Results may differ from the reference program's by a relative error of at most 0.025.
The reference program's roundings to bfloat16 on the way count: a program that leaves them out, or rounds other values in their place, can miss the bound.
Values may be sent and summed in bfloat16 or wider, within the bound.
No kernel may reach another device: no remote copies, remote signals or barrier semaphores. Data moves between devices by JAX's collectives and lax.ppermute only.
A program may use at most 128 MiB of HBM per device.

```python
import math
import jax
import jax.numpy as jnp
from jax import lax

QUERY_HEADS = 32
KEY_VALUE_HEADS = 16
HEAD_SIZE = 128
WINDOW = 1024
TOKENS_PER_SHARD = 512
SLABS = 4
DOCS = 8
TOTAL_TOKENS = 4096
LENGTH = 1024


def scaled_gaussian(key, count_rows, columns):
    noise_key, row_key, column_key = jax.random.split(key, 3)
    noise_rows = jnp.clip(jax.random.normal(noise_key, (count_rows, columns), jnp.float32), -6.0, 6.0)
    row_scale = jnp.exp(jax.random.uniform(row_key, (count_rows, 1), jnp.float32, 0.0, math.log(10.0)))
    column_scale = jnp.exp(jax.random.uniform(column_key, (1, columns), jnp.float32, 0.0, math.log(10.0)))
    return noise_rows * row_scale * column_scale


def key_provider(key):
    return scaled_gaussian(jax.random.fold_in(key, 11), TOTAL_TOKENS, KEY_VALUE_HEADS * HEAD_SIZE)


def draw_key_before_norm(key, part):
    return key_provider(key).astype(jnp.bfloat16)


def draw_query_raw(key, part):
    values = scaled_gaussian(jax.random.fold_in(key, 23), TOTAL_TOKENS, QUERY_HEADS * HEAD_SIZE)
    return values.astype(jnp.bfloat16)


def draw_query_gain(key, part):
    gain_key = jax.random.fold_in(key, 41)
    return jax.random.uniform(gain_key, (HEAD_SIZE,), jnp.float32, 0.5, 2.0)


def draw_key_norm_gain(key, part):
    gain_key = jax.random.fold_in(key, 43)
    return jax.random.uniform(gain_key, (HEAD_SIZE,), jnp.float32, 0.5, 2.0)


def slab_starts(slab_key):
    picked = jax.random.permutation(slab_key, LENGTH - 2)[:DOCS - 1].astype(jnp.int32) + 1
    picked = jnp.where(picked >= LENGTH // 2, picked + 1, picked)
    return jnp.sort(picked)


def draw_doc_starts(key, part):
    keys_list = jax.random.split(jax.random.fold_in(key, 53), SLABS)
    inner = jax.vmap(slab_starts)(keys_list)
    inner = inner.at[0, DOCS - 2].set(LENGTH - 1)
    return jnp.concatenate([jnp.zeros((SLABS, 1), jnp.int32), inner], axis=1).astype(jnp.int32)


def draw_windows(key, part):
    width_key, slot_key = jax.random.split(jax.random.fold_in(key, 61))
    widths = jax.random.randint(width_key, (SLABS,), WINDOW // 2 + 1, WINDOW + 1)
    chosen = jax.random.randint(slot_key, (), 0, SLABS)
    return jnp.where(jnp.arange(SLABS) == chosen, WINDOW, widths).astype(jnp.int32)


def shard_levels(key, dims, cuts, least, largest):
    level, own = 1.0, jax.random.fold_in(key, 6)
    for dim, parts in cuts:
        draws = jnp.exp(jax.random.uniform(jax.random.fold_in(own, dim), (parts,), jnp.float32, least / len(cuts), largest / len(cuts)))
        level = level * jnp.repeat(draws, dims[dim] // parts).reshape([-1 if axis == dim else 1 for axis in range(len(dims))])
    return level


def gaussian(key, dims, scale, limit, pieces=(), kind=jnp.bfloat16):
    factor_of = shard_levels(key, dims, pieces, -0.22, 0.18) if pieces else 1.0
    values = jax.random.normal(key, dims, jnp.float32) * scale * factor_of
    return jnp.minimum(jnp.maximum(values, -limit), limit).astype(kind)


def setup_inputs(seed: int = 0) -> dict:
    seeds = jax.random.split(jax.random.key(seed), 9)
    return {
        "query_raw": draw_query_raw(jax.random.fold_in(seeds[8], 71), 0),
        "key_before_norm": draw_key_before_norm(jax.random.fold_in(seeds[8], 71), 0),
        "value_input": gaussian(seeds[2], (TOTAL_TOKENS, KEY_VALUE_HEADS * HEAD_SIZE), 1.0, 6.0, ((0, 8), (1, 4))),
        "out_cotangent": gaussian(seeds[3], (TOTAL_TOKENS, QUERY_HEADS * HEAD_SIZE), 1.0, 6.0, ((0, 8), (1, 4))),
        "query_gain": draw_query_gain(jax.random.fold_in(seeds[8], 71), 0),
        "key_norm_gain": draw_key_norm_gain(jax.random.fold_in(seeds[8], 71), 0),
        "doc_starts": draw_doc_starts(jax.random.fold_in(seeds[8], 71), 0),
        "windows": draw_windows(jax.random.fold_in(seeds[8], 71), 0),
    }


score_scale = 168.0 ** (-0.5)
norm_eps = 1e-06
masked_score = -1e+30

def token_info(token_ids, doc_starts, windows, slab_length, total_tokens):
    placed = (token_ids + total_tokens - slab_length // 2) % total_tokens
    slab_id = placed // slab_length
    in_slab = placed - slab_id * slab_length
    one_hot = (jnp.arange(windows.shape[0], dtype=jnp.int32)[None, :] == slab_id[:, None]).astype(jnp.int32)
    row_starts = lax.optimization_barrier(jnp.sum(one_hot[:, :, None] * doc_starts[None, :, :], axis=1))
    reached = row_starts <= in_slab[:, None]
    doc_count = lax.optimization_barrier(jnp.sum(reached.astype(jnp.int32), axis=1))
    doc_begin = lax.optimization_barrier(jnp.max(jnp.where(reached, row_starts, 0), axis=1))
    doc_id = slab_id * doc_starts.shape[1] + doc_count
    win_size = lax.optimization_barrier(jnp.sum(one_hot * windows[None, :], axis=1))
    return (doc_id, in_slab, in_slab - doc_begin, win_size)

def rope_tables(rope_pos, head_dim):
    half_dim = head_dim // 2
    spacing = jnp.arange(half_dim, dtype=jnp.float32) * (2.0 / head_dim)
    inverse_freq = 10000.0 ** (-spacing)
    angle = rope_pos.astype(jnp.float32)[:, None] * inverse_freq[None, :]
    return (jnp.cos(angle)[:, None, :], jnp.sin(angle)[:, None, :])

def apply_norm(raw_rows, gain_vec, cosine_table, sine_table):
    floats = raw_rows.astype(jnp.float32)
    inverse = lax.rsqrt(lax.optimization_barrier(jnp.mean(floats * floats, axis=-1)) + norm_eps)
    scaled = floats * inverse[..., None] * gain_vec
    half_dim = scaled.shape[-1] // 2
    low_half, high_half = (scaled[..., :half_dim], scaled[..., half_dim:])
    turned = jnp.concatenate([low_half * cosine_table - high_half * sine_table, high_half * cosine_table + low_half * sine_table], axis=-1)
    return (turned.astype(jnp.bfloat16), floats, inverse)

def norm_backward(grad_hat, floats, inverse, gain_vec, cosine_table, sine_table):
    half_dim = grad_hat.shape[-1] // 2
    low_half, high_half = (grad_hat[..., :half_dim], grad_hat[..., half_dim:])
    grad_scaled = jnp.concatenate([low_half * cosine_table + high_half * sine_table, high_half * cosine_table - low_half * sine_table], axis=-1)
    unit_rows = floats * inverse[..., None]
    gain_grad = lax.optimization_barrier(jnp.sum(grad_scaled * unit_rows, axis=(0, 1)))
    weighted = grad_scaled * gain_vec
    correction = lax.optimization_barrier(jnp.mean(weighted * floats, axis=-1))
    grad_raw = inverse[..., None] * weighted - floats * (inverse * inverse * inverse * correction)[..., None]
    return (grad_raw, gain_grad)

def reference(query_raw, key_before_norm, value_input, out_cotangent, query_gain, key_norm_gain, doc_starts, windows):
    group_width = QUERY_HEADS // KEY_VALUE_HEADS
    reach_shards = (WINDOW - 1) // TOKENS_PER_SHARD + 1
    window_margin = reach_shards * TOKENS_PER_SHARD
    key_span = window_margin + TOKENS_PER_SHARD
    token_ids = jnp.arange(TOTAL_TOKENS, dtype=jnp.int32)
    doc_id, in_slab, rope_pos, win_size = token_info(token_ids, doc_starts, windows, LENGTH, TOTAL_TOKENS)
    cosine_table, sine_table = rope_tables(rope_pos, HEAD_SIZE)
    query_unit, query_float, query_inverse = apply_norm(query_raw.reshape(TOTAL_TOKENS, QUERY_HEADS, HEAD_SIZE), query_gain, cosine_table, sine_table)
    key_unit, key_single, key_inverse_norm = apply_norm(key_before_norm.reshape(TOTAL_TOKENS, KEY_VALUE_HEADS, HEAD_SIZE), key_norm_gain, cosine_table, sine_table)
    value_row_block = value_input.reshape(TOTAL_TOKENS, KEY_VALUE_HEADS, HEAD_SIZE)
    gradient_rows = out_cotangent.reshape(TOTAL_TOKENS, QUERY_HEADS, HEAD_SIZE)
    tail_start = TOTAL_TOKENS - window_margin
    key_with_padding = jnp.concatenate([key_unit[tail_start:], key_unit], 0)
    value_with_padding = jnp.concatenate([value_row_block[tail_start:], value_row_block], 0)
    doc_padded = jnp.concatenate([doc_id[tail_start:], doc_id], 0)
    slab_padded = jnp.concatenate([in_slab[tail_start:], in_slab], 0)

    def block_step(running, block_id):
        key_acc, value_accumulator = running
        first_row = (block_id * TOKENS_PER_SHARD).astype(jnp.int32)
        query_tile = lax.dynamic_slice_in_dim(query_unit, first_row, TOKENS_PER_SHARD, 0).reshape(TOKENS_PER_SHARD, KEY_VALUE_HEADS, group_width, HEAD_SIZE).astype(jnp.float32)
        gradient_block = lax.dynamic_slice_in_dim(gradient_rows, first_row, TOKENS_PER_SHARD, 0).reshape(TOKENS_PER_SHARD, KEY_VALUE_HEADS, group_width, HEAD_SIZE).astype(jnp.float32)
        block_doc = lax.dynamic_slice_in_dim(doc_id, first_row, TOKENS_PER_SHARD, 0)
        block_slab = lax.dynamic_slice_in_dim(in_slab, first_row, TOKENS_PER_SHARD, 0)
        block_window = lax.dynamic_slice_in_dim(win_size, first_row, TOKENS_PER_SHARD, 0)
        key_block = lax.dynamic_slice_in_dim(key_with_padding, first_row, key_span, 0).astype(jnp.float32)
        value_block = lax.dynamic_slice_in_dim(value_with_padding, first_row, key_span, 0).astype(jnp.float32)
        near_doc = lax.dynamic_slice_in_dim(doc_padded, first_row, key_span, 0)
        near_slab = lax.dynamic_slice_in_dim(slab_padded, first_row, key_span, 0)
        pos_gap = block_slab[:, None] - near_slab[None, :]
        visible = (block_doc[:, None] == near_doc[None, :]) & (pos_gap >= 0) & (pos_gap < block_window[:, None])
        scores = jnp.einsum('rhgd,khd->hgrk', query_tile, key_block) * score_scale
        scores = jnp.where(visible[None, None], scores, masked_score)
        row_max = lax.optimization_barrier(jnp.max(scores, axis=-1, keepdims=True))
        exponent = jnp.exp(scores - row_max)
        row_sum = lax.optimization_barrier(jnp.sum(exponent, axis=-1, keepdims=True))
        softmax = exponent / row_sum
        grad_soft = jnp.einsum('rhgd,khd->hgrk', gradient_block, value_block)
        row_delta = lax.optimization_barrier(jnp.sum(softmax * grad_soft, axis=-1, keepdims=True))
        grad_scores = lax.optimization_barrier((softmax * (grad_soft - row_delta)).astype(jnp.bfloat16)).astype(jnp.float32)
        soft_half = lax.optimization_barrier(softmax.astype(jnp.bfloat16)).astype(jnp.float32)
        grad_query = score_scale * jnp.einsum('hgrk,khd->rhgd', grad_scores, key_block)
        grad_key = score_scale * jnp.einsum('hgrk,rhgd->khd', grad_scores, query_tile)
        grad_value = jnp.einsum('hgrk,rhgd->khd', soft_half, gradient_block)
        key_acc = lax.dynamic_update_slice_in_dim(key_acc, lax.dynamic_slice_in_dim(key_acc, first_row, key_span, 0) + grad_key, first_row, 0)
        value_accumulator = lax.dynamic_update_slice_in_dim(value_accumulator, lax.dynamic_slice_in_dim(value_accumulator, first_row, key_span, 0) + grad_value, first_row, 0)
        return ((key_acc, value_accumulator), grad_query.reshape(TOKENS_PER_SHARD, QUERY_HEADS, HEAD_SIZE))
    initial_accumulator = jnp.zeros((TOTAL_TOKENS + window_margin, KEY_VALUE_HEADS, HEAD_SIZE), jnp.float32)
    (key_acc, value_accumulator), grad_query = lax.scan(block_step, (initial_accumulator, initial_accumulator), jnp.arange(TOTAL_TOKENS // TOKENS_PER_SHARD, dtype=jnp.int32))
    grad_query_hat = grad_query.reshape(TOTAL_TOKENS, QUERY_HEADS, HEAD_SIZE)
    grad_key_hat = key_acc[window_margin:].at[tail_start:].add(key_acc[:window_margin])
    value_total = value_accumulator[window_margin:].at[tail_start:].add(value_accumulator[:window_margin])
    query_gradient, query_norm_gain_gradient = norm_backward(grad_query_hat, query_float, query_inverse, query_gain, cosine_table, sine_table)
    key_gradient, key_norm_gain_gradient = norm_backward(grad_key_hat, key_single, key_inverse_norm, key_norm_gain, cosine_table, sine_table)
    value_gradient = value_total.reshape(TOTAL_TOKENS, KEY_VALUE_HEADS * HEAD_SIZE).astype(jnp.bfloat16)
    return (query_gradient.reshape(TOTAL_TOKENS, QUERY_HEADS * HEAD_SIZE).astype(jnp.bfloat16), key_gradient.reshape(TOTAL_TOKENS, KEY_VALUE_HEADS * HEAD_SIZE).astype(jnp.bfloat16), value_gradient, query_norm_gain_gradient, key_norm_gain_gradient)
```

```python
import functools

import jax
import jax.numpy as jnp
from jax import lax
from jax.experimental import pallas as pl
from jax.experimental.pallas import tpu as pltpu
from jax.sharding import PartitionSpec as P

WINDOW = 1024
SLABS = 4

score_scale = 168.0 ** (-0.5)
log2_e = 1.4426950408889634
norm_eps = 1e-06
masked_score = -1e30
exp_scale = score_scale * log2_e

TILE = 128
STRIP = 32


def dot(a, b, contract):
    return lax.dot_general(a, b, ((contract[:1], contract[1:]), ((), ())), preferred_element_type=jnp.float32)


def inverse_rms(floats):
    return lax.rsqrt(jnp.mean(floats * floats, axis=-1, keepdims=True) + norm_eps)


def norm_forward(raw, gain, cosine, sine):
    floats = raw.astype(jnp.float32)
    scaled = floats * inverse_rms(floats) * gain
    turned = scaled * cosine + pltpu.roll(scaled, scaled.shape[1] // 2, 1) * sine
    return turned.astype(jnp.bfloat16)


def norm_backward(turned, raw, gain):
    floats = raw.astype(jnp.float32)
    inverse = inverse_rms(floats)
    gain_grad = jnp.sum((turned * (floats * inverse)).reshape(-1, 8, turned.shape[1]), axis=0)
    weighted = turned * gain
    correction = jnp.mean(weighted * floats, axis=-1, keepdims=True)
    return inverse * weighted - floats * (inverse * inverse * inverse * correction), gain_grad


def attention_kernel(reach, chained, docs, index, place, meta, *refs):
    refs = list(refs)[1 if chained else 0 :]
    gains_ref, cos_ref, sin_ref, turned_ref, q_ref, do_ref, k_all, v_all = refs[:8]
    far_refs = refs[8 : 8 + reach]
    refs = refs[8 + reach :]
    dq_out, kgrad_ref, vgrad_ref = refs[:3]
    back_refs = refs[3 : 3 + reach]
    gain_out = refs[3 + reach]
    score_buf, soft_grad_buf, soft_buf, ds_buf, k_hat, v_buf, k_turned, q_hat, do_buf, dk_acc, dv_acc, dq_buf, gain_acc, dq_ref, dq_sem = refs[
        4 + reach :
    ]
    rows = q_ref.shape[0]
    head = gains_ref.shape[1]
    half = head // 2
    group = q_ref.shape[1] // k_all.shape[1]
    tile = TILE
    lanes = group * tile
    tiles = rows // tile
    far_rows = reach * rows
    all_keys = far_rows + rows
    base, window = meta[0], meta[1]
    origin = base - far_rows
    own = slice(index * head, (index + 1) * head)
    far_key = slice(2 * place * head, (2 * place + 1) * head)
    far_value = slice((2 * place + 1) * head, (2 * place + 2) * head)
    sources = [(far_refs[d - 1].at[:, far_key], far_refs[d - 1].at[:, far_value], d * rows) for d in range(reach, 0, -1)]
    sources.append((k_all.at[:, own], v_all.at[:, own], 0))
    q_gain, k_gain = gains_ref[0:1, :], gains_ref[1:2, :]
    gain_acc[...] = jnp.zeros_like(gain_acc)

    def first_visible(position, zero):
        first = zero
        for j in range(docs):
            start = meta[2 + j]
            first = jnp.maximum(first, jnp.where(position >= start, start, 0))
        return jnp.maximum(first, position - window + 1)

    def aligned(value):
        return pl.multiple_of(value, tile)

    start_row = first_visible(base, 0) - origin

    def key_forward(block, step):
        raw, value, table = sources[block]
        lo = aligned(step * tile)
        at = pl.ds(aligned(table + lo), tile)
        to = aligned(block * rows + lo)
        v_buf[pl.ds(to, tile)] = value[pl.ds(lo, tile)]
        dk_acc[pl.ds(to, tile)] = jnp.zeros((tile, head), jnp.float32)
        dv_acc[pl.ds(to, tile)] = jnp.zeros((tile, head), jnp.float32)
        hat = norm_forward(raw[pl.ds(lo, tile)], k_gain, cos_ref[at], sin_ref[at])
        k_hat[pl.ds(to, tile)] = hat
        k_turned[:, pl.ds(to, tile)] = jnp.transpose(hat)

    def key_hidden(block, step):
        to = aligned(block * rows + step * tile)
        v_buf[pl.ds(to, tile)] = jnp.zeros((tile, head), jnp.bfloat16)
        dk_acc[pl.ds(to, tile)] = jnp.zeros((tile, head), jnp.float32)
        dv_acc[pl.ds(to, tile)] = jnp.zeros((tile, head), jnp.float32)
        k_hat[pl.ds(to, tile)] = jnp.zeros((tile, head), jnp.bfloat16)
        k_turned[:, pl.ds(to, tile)] = jnp.zeros((head, tile), jnp.bfloat16)

    def key_backward(block, step):
        raw, _, table = sources[block]
        lo = aligned(step * tile)
        inner = pl.ds(lo, tile)
        at = pl.ds(aligned(table + lo), tile)
        sel = pl.ds(aligned(block * rows + lo), tile)
        dk = dk_acc[sel] * score_scale
        turned = dk * cos_ref[at] - pltpu.roll(dk, half, 1) * sin_ref[at]
        raw_grad, gain_part = norm_backward(turned, raw[inner], k_gain)
        gain_acc[8:16] += gain_part
        if block == reach:
            kgrad_ref[inner, :] = raw_grad
            vgrad_ref[inner, :] = dv_acc[sel]
        else:
            back = back_refs[reach - block - 1]
            back[inner, :head] = raw_grad.astype(jnp.bfloat16)
            back[inner, head:] = dv_acc[sel].astype(jnp.bfloat16)

    def key_unused(block, step):
        lo = aligned(step * tile)
        back_refs[reach - block - 1][pl.ds(lo, tile)] = jnp.zeros((tile, 2 * head), jnp.bfloat16)

    def over_keys(used, unused):
        for block in range(reach + 1):
            first = jnp.clip((start_row - block * rows) // tile, 0, tiles) if block < reach else 0
            if block < reach:
                lax.fori_loop(0, first, lambda step, _: unused(block, step), None)
            lax.fori_loop(first, tiles, lambda step, _: used(block, step), None)

    def query_forward(n, _):
        here = pl.ds(aligned(n * tile), tile)
        cos, sin = cos_ref[here], sin_ref[here]
        for g in range(group):
            cols = slice((index * group + g) * head, (index * group + g + 1) * head)
            to = pl.ds(aligned(n * lanes + g * tile), tile)
            q_hat[to] = norm_forward(q_ref[here, cols], q_gain, cos, sin)
            do_buf[to] = do_ref[here, cols]

    def query_backward(n, _):
        here = pl.ds(aligned(n * tile), tile)
        for g in range(group):
            cols = slice((index * group + g) * head, (index * group + g + 1) * head)
            at = pl.ds(aligned(n * lanes + g * tile), tile)
            raw_grad, gain_part = norm_backward(dq_buf[at], q_ref[here, cols], q_gain)
            gain_acc[0:8] += gain_part
            dq_ref[here, g * head : (g + 1) * head] = raw_grad.astype(jnp.bfloat16)

    def tile_step(n, length, begin):
        lo = aligned(n * tile)
        here = pl.ds(lo, tile)
        at_q = pl.ds(aligned(n * lanes), lanes)
        keys = pl.ds(begin, length)
        query_pos = base + lo + lax.broadcasted_iota(jnp.int32, (1, tile), 1)
        lower = first_visible(query_pos, jnp.zeros_like(query_pos)) - (origin + begin)
        lower = jnp.concatenate([lower] * group, 1)
        upper = jnp.concatenate([query_pos - (origin + begin)] * group, 1)
        offset = lax.broadcasted_iota(jnp.int32, (STRIP, lanes), 0)
        strips = range(0, length, STRIP)

        def fold(values):
            return values.reshape(STRIP // 8, 8, lanes)

        score_buf[:length] = dot(k_hat[keys], q_hat[at_q], (1, 1))
        soft_grad_buf[:length] = dot(v_buf[keys], do_buf[at_q], (1, 1))
        top = jnp.full((8, lanes), masked_score, jnp.float32)
        for at in strips:
            visible = offset >= lower - at
            if length == all_keys or at + STRIP > length - tile:
                visible &= offset <= upper - at
            part = jnp.where(visible, score_buf[at : at + STRIP], masked_score)
            score_buf[at : at + STRIP] = part
            top = jnp.maximum(top, jnp.max(fold(part), axis=0))
        top = jnp.max(top, axis=0, keepdims=True) * exp_scale
        total = jnp.zeros((8, lanes), jnp.float32)
        product = jnp.zeros((8, lanes), jnp.float32)
        for at in strips:
            sel = slice(at, at + STRIP)
            weight = jnp.exp2(score_buf[sel] * exp_scale - top)
            score_buf[sel] = weight
            total += jnp.sum(fold(weight), axis=0)
            product += jnp.sum(fold(weight * soft_grad_buf[sel]), axis=0)
        recip = 1.0 / jnp.sum(total, axis=0, keepdims=True)
        delta = jnp.sum(product, axis=0, keepdims=True) * recip
        for at in strips:
            sel = slice(at, at + STRIP)
            soft = score_buf[sel] * recip
            soft_buf[sel] = soft.astype(jnp.bfloat16)
            ds_buf[sel] = (soft * (soft_grad_buf[sel] - delta)).astype(jnp.bfloat16)
        grad = dot(k_turned[:, keys], ds_buf[:length], (1, 0)) * score_scale
        dk_acc[keys] += dot(ds_buf[:length], q_hat[at_q], (1, 0))
        dv_acc[keys] += dot(soft_buf[:length], do_buf[at_q], (1, 0))
        low, high = grad[:half], grad[half:]
        cos = jnp.concatenate([turned_ref[:half, here]] * group, 1)
        sin = jnp.concatenate([turned_ref[half:, here]] * group, 1)
        dq_buf[at_q] = jnp.transpose(jnp.concatenate([low * cos + high * sin, high * cos - low * sin], 0))

    def query_tile(n, _):
        end = far_rows + (n + 1) * tile
        need = end - (first_visible(base + n * tile, 0) - origin)
        lengths = [length for length in (2 * tile, 4 * tile) if length <= far_rows] + [all_keys]
        for shorter, length in zip([0] + lengths, lengths):
            begin = 0 if length == all_keys else aligned(end - length)
            body = functools.partial(tile_step, n, length, begin)
            if length == all_keys:
                pl.when(need > shorter)(body)
            else:
                pl.when((need > shorter) & (need <= length))(body)

    over_keys(key_forward, key_hidden)
    lax.fori_loop(0, tiles, query_forward, None)
    lax.fori_loop(0, tiles, query_tile, None)
    lax.fori_loop(0, tiles, query_backward, None)
    mine = dq_out.at[:, index * group * head : (index + 1) * group * head]
    copy = pltpu.make_async_copy(dq_ref, mine, dq_sem)
    copy.start()
    over_keys(key_backward, key_unused)
    copy.wait()
    gain_out[0:1, :] = jnp.sum(gain_acc[0:8], axis=0, keepdims=True)
    gain_out[1:2, :] = jnp.sum(gain_acc[8:16], axis=0, keepdims=True)


def attention(meta, gains, cos, sin, turned, q, do, k, v, far, place, carried, index, docs, cost):
    rows = q.shape[0]
    head = gains.shape[1]
    group = q.shape[1] // k.shape[1]
    reach = len(far)
    operands = [meta, gains, cos, sin, turned, q, do, k, v, *far]
    aliases = {}
    if carried is not None:
        aliases = {1: 0}
        operands.insert(1, carried)
    keys = (reach + 1) * rows
    lanes = group * TILE
    out_shape = [jax.ShapeDtypeStruct(q.shape, jnp.bfloat16)]
    out_shape += [jax.ShapeDtypeStruct((rows, head), jnp.float32)] * 2
    out_shape += [jax.ShapeDtypeStruct((rows, 2 * head), jnp.bfloat16)] * reach
    out_shape += [jax.ShapeDtypeStruct((2, head), jnp.float32)]
    in_vmem = pl.BlockSpec(memory_space=pltpu.VMEM)
    return pl.pallas_call(
        functools.partial(attention_kernel, reach, carried is not None, docs, index, place),
        in_specs=[pl.BlockSpec(memory_space=pltpu.SMEM)]
        + [pl.BlockSpec(memory_space=pl.ANY)] * len(aliases)
        + [in_vmem] * (len(operands) - 1 - len(aliases)),
        out_specs=[pl.BlockSpec(memory_space=pl.ANY)] + [in_vmem] * (len(out_shape) - 1),
        scratch_shapes=[pltpu.VMEM((keys, lanes), jnp.float32)] * 2
        + [pltpu.VMEM((keys, lanes), jnp.bfloat16)] * 2
        + [pltpu.VMEM((keys, head), jnp.bfloat16)] * 2
        + [pltpu.VMEM((head, keys), jnp.bfloat16)]
        + [pltpu.VMEM((group * rows, head), jnp.bfloat16)] * 2
        + [pltpu.VMEM((keys, head), jnp.float32)] * 2
        + [pltpu.VMEM((group * rows, head), jnp.float32), pltpu.VMEM((16, head), jnp.float32)]
        + [pltpu.VMEM((rows, group * head), jnp.bfloat16), pltpu.SemaphoreType.DMA],
        out_shape=out_shape,
        input_output_aliases=aliases,
        compiler_params=pltpu.CompilerParams(vmem_limit_bytes=24 * 1024 * 1024),
        cost_estimate=pl.CostEstimate(flops=cost, bytes_accessed=1, transcendentals=0),
    )(*operands)


def join_kernel(reach, own_key, own_value, *refs):
    head = own_key.shape[1]
    key_out, value_out = refs[-2:]
    key, value = own_key[...], own_value[...]
    for back in refs[:reach]:
        block = back[...].astype(jnp.float32)
        key = key + block[:, :head]
        value = value + block[:, head:]
    key_out[...] = key.astype(jnp.bfloat16)
    value_out[...] = value.astype(jnp.bfloat16)


def join(own, back, carried, first, like, cost):
    rows = like.shape[0]
    head = own[0].shape[1]
    reach = len(back)
    local = lambda j: (0, j)
    column = lambda j: (0, first + j)
    operands = [*own, *back]
    in_specs = [pl.BlockSpec((rows, head), local)] * 2 + [pl.BlockSpec((rows, 2 * head), local)] * reach
    aliases = {}
    if carried is not None:
        aliases = {len(operands): 0, len(operands) + 1: 1}
        operands += carried
        in_specs += [pl.BlockSpec(memory_space=pl.ANY)] * 2
    return pl.pallas_call(
        functools.partial(join_kernel, reach),
        grid=(1,),
        in_specs=in_specs,
        out_specs=[pl.BlockSpec((rows, head), column)] * 2,
        out_shape=[jax.ShapeDtypeStruct(like.shape, like.dtype)] * 2,
        input_output_aliases=aliases,
        compiler_params=pltpu.CompilerParams(vmem_limit_bytes=8 * 1024 * 1024),
        cost_estimate=pl.CostEstimate(flops=1, bytes_accessed=cost, transcendentals=0),
    )(*operands)


def shards(
    query_raw, key_before_norm, value_input, out_cotangent, query_gain, key_norm_gain, doc_starts, windows
):
    rows = query_raw.shape[0]
    head = query_gain.shape[0]
    key_heads = key_before_norm.shape[1] // head
    shard_count = lax.axis_size("seq")
    slab_shards = shard_count // SLABS
    slab_length = slab_shards * rows
    shift = slab_length // 2 // rows
    assert slab_shards * SLABS == shard_count and shift * rows * 2 == slab_length
    reach = min((WINDOW - 1) // rows + 1, slab_shards - 1)
    docs = doc_starts.shape[1]

    def links(distance):
        found = []
        for i in range(shard_count):
            if (i - shift) % slab_shards + distance < slab_shards:
                found.append((i, (i + distance) % shard_count))
        return found

    firsts = [0, 1, 2, key_heads] if key_heads > 2 else [0, key_heads]
    far = []
    for first, last in zip(firsts, firsts[1:]):
        cols = [slice(j * head, (j + 1) * head) for j in range(first, last)]
        packed = jnp.concatenate([a[:, c] for c in cols for a in (key_before_norm, value_input)], 1)
        blocks = [lax.ppermute(packed, "seq", links(d)) for d in range(1, reach + 1)]
        far += [(blocks, place) for place in range(last - first)]

    placed = (lax.axis_index("seq") - shift) % shard_count
    slab = placed // slab_shards
    base = (placed % slab_shards) * rows
    starts = lax.dynamic_index_in_dim(doc_starts, slab, 0, keepdims=False)
    window = lax.dynamic_index_in_dim(windows, slab, 0, keepdims=True)
    meta = jnp.concatenate([base[None], window, starts]).astype(jnp.int32)
    positions = jnp.concatenate(
        [base - d * rows + jnp.arange(rows, dtype=jnp.int32) for d in range(reach + 1)]
    )
    begins = jnp.max(jnp.where(starts[None, :] <= positions[:, None], starts[None, :], 0), axis=1)
    spacing = jnp.arange(head // 2, dtype=jnp.float32) * (2.0 / head)
    angle = (positions - begins).astype(jnp.float32)[:, None] * (10000.0 ** (-spacing))[None, :]
    cosine, sine = jnp.cos(angle), jnp.sin(angle)
    cos_table = jnp.concatenate([cosine, cosine], axis=1)
    sin_table = jnp.concatenate([-sine, sine], axis=1)
    across = (10000.0 ** (-spacing))[:, None] * (positions - begins)[:rows].astype(jnp.float32)[None, :]
    turned = jnp.concatenate([jnp.cos(across), jnp.sin(across)], axis=0)
    gains = jnp.stack([query_gain, key_norm_gain])

    query_gradient = None
    owns, backs, gain_parts = [], [], []
    for j, (blocks, place) in enumerate(far):
        if j >= 2:
            meta, backs[j - 2] = lax.optimization_barrier((meta, backs[j - 2]))
        out = attention(
            meta, gains, cos_table, sin_table, turned, query_raw, out_cotangent, key_before_norm, value_input,
            blocks, place, query_gradient, j, docs, 10**10 if j >= 2 else 1,
        )
        query_gradient = out[0]
        owns.append(out[1:3])
        gain_parts.append(out[-1])
        backs.append([
            lax.ppermute(back, "seq", [(b, a) for a, b in links(d)]) for d, back in enumerate(out[3:-1], 1)
        ])
    gain_sum = sum(gain_parts)
    if len(backs) > 1:
        gain_sum, backs[-2] = lax.optimization_barrier((gain_sum, backs[-2]))
    everyone = jnp.broadcast_to(gain_sum, (shard_count * lax.axis_size("head"), 2, head))
    gathered = lax.all_to_all(everyone, ("seq", "head"), 0, 0)
    carried = None
    for j, (own, back) in enumerate(zip(owns, backs)):
        carried = join(own, back, carried, j, key_before_norm, 1 if j + 1 < key_heads else 200 * 10**6)
    total = jnp.sum(gathered, axis=0)
    return query_gradient, *carried, total[0], total[1]


def solution(mesh):
    placed = (P("seq", "head"),) * 4 + (P(),) * 4
    return jax.shard_map(
        shards,
        mesh=mesh,
        in_specs=placed,
        out_specs=(P("seq", "head"), P("seq", "head"), P("seq", "head"), P(), P()),
        check_vma=False,
    )
```

```python
import functools

import jax
import jax.numpy as jnp
from jax import lax
from jax.experimental import pallas as pl
from jax.experimental.pallas import tpu as pltpu
from jax.sharding import PartitionSpec as P

WINDOW = 1024
SLABS = 4

score_scale = 168.0 ** (-0.5)
log2_e = 1.4426950408889634
norm_eps = 1e-06
masked_score = -1e30
exp_scale = score_scale * log2_e

TILE = 128
STRIP = 32


def dot(a, b, contract):
    return lax.dot_general(a, b, ((contract[:1], contract[1:]), ((), ())), preferred_element_type=jnp.float32)


def inverse_rms(floats):
    return lax.rsqrt(jnp.mean(floats * floats, axis=-1, keepdims=True) + norm_eps)


def norm_forward(raws, gain, cosine, sine):
    floats = [raw.astype(jnp.float32) for raw in raws]
    inverses = [inverse_rms(f) for f in floats]
    scaled = [f * i * gain for f, i in zip(floats, inverses)]
    rolled = [pltpu.roll(s, s.shape[1] // 2, 1) for s in scaled]
    return [(s * cosine + r * sine).astype(jnp.bfloat16) for s, r in zip(scaled, rolled)]


def norm_backward(turned, raws, gain):
    floats = [raw.astype(jnp.float32) for raw in raws]
    inverses = [inverse_rms(f) for f in floats]
    weighted = [t * gain for t in turned]
    corrections = [jnp.mean(w * f, axis=-1, keepdims=True) for w, f in zip(weighted, floats)]
    gain_grad = sum(
        jnp.sum((t * (f * i)).reshape(-1, 8, t.shape[1]), axis=0) for t, f, i in zip(turned, floats, inverses)
    )
    grads = [
        i * w - f * (i * i * i * c) for f, i, w, c in zip(floats, inverses, weighted, corrections)
    ]
    return grads, gain_grad


def aligned(value):
    return pl.multiple_of(value, TILE)


def in_batches(items, size):
    return [items[n : n + size] for n in range(0, len(items), size)]


def columns(j, head):
    return slice(j * head, (j + 1) * head)


def prepare_kernel(gains_ref, cos_ref, sin_ref, q_ref, k_ref, q_hat, k_hat, k_turned):
    rows = q_ref.shape[0]
    head = gains_ref.shape[1]

    def step(n, _):
        here = pl.ds(aligned(n * TILE), TILE)
        cos, sin = cos_ref[here], sin_ref[here]
        for raw, row, out in ((q_ref, 0, q_hat), (k_ref, 1, k_hat)):
            for batch in in_batches(range(raw.shape[1] // head), 4):
                hats = norm_forward([raw[here, columns(j, head)] for j in batch], gains_ref[row : row + 1], cos, sin)
                for j, hat in zip(batch, hats):
                    out[here, columns(j, head)] = hat
                    if row == 1:
                        k_turned[columns(j, head), here] = jnp.transpose(hat)

    lax.fori_loop(0, rows // TILE, step, None)


def prepare(gains, cos, sin, q, k):
    in_vmem = pl.BlockSpec(memory_space=pltpu.VMEM)
    return pl.pallas_call(
        prepare_kernel,
        in_specs=[in_vmem] * 5,
        out_specs=[in_vmem] * 3,
        out_shape=[jax.ShapeDtypeStruct(shape, jnp.bfloat16) for shape in (q.shape, k.shape, k.shape[::-1])],
        compiler_params=pltpu.CompilerParams(vmem_limit_bytes=16 * 1024 * 1024),
        cost_estimate=pl.CostEstimate(flops=1, bytes_accessed=1, transcendentals=0),
    )(gains, cos, sin, q, k)


def attention_kernel(reach, docs, first_head, count, meta, *refs):
    gains_ref, cos_ref, sin_ref, q_hat, k_own, k_own_turned, do_ref, v_all = refs[:8]
    far_refs = refs[8 : 8 + reach]
    refs = refs[8 + reach :]
    dq_out, dk_out, dv_out = refs[:3]
    back_refs = refs[3 : 3 + reach]
    gain_out = refs[3 + reach]
    score_buf, soft_grad_buf, soft_buf, ds_buf, k_hat, v_buf, k_turned, dk_acc, dv_acc, gain_acc = refs[4 + reach :]
    rows = q_hat.shape[0]
    head = gains_ref.shape[1]
    half = head // 2
    group = q_hat.shape[1] // k_own.shape[1]
    tile = 2 * TILE
    lanes = group * tile
    tiles = rows // tile
    far_rows = reach * rows
    all_keys = far_rows + rows
    base, window = meta[0], meta[1]
    origin = base - far_rows
    k_gain = gains_ref[1:2, :]
    gain_acc[...] = jnp.zeros_like(gain_acc)

    def first_visible(position, zero):
        first = zero
        for j in range(docs):
            start = meta[2 + j]
            first = jnp.maximum(first, jnp.where(position >= start, start, 0))
        return jnp.maximum(first, position - window + 1)

    start_row = first_visible(base, 0) - origin

    def lanes_of(j):
        return pl.ds(aligned(j * head), head)

    def source(h, block, lo):
        far = far_refs[reach - block - 1]
        at = pl.ds(lo, tile)
        table = pl.ds(aligned((reach - block) * rows + lo), tile)
        return far[at, lanes_of(h)], far[at, lanes_of(count + h)], cos_ref[table], sin_ref[table]

    def key_forward(h, block, step):
        lo = aligned(step * tile)
        to = pl.ds(aligned(block * rows + lo), tile)
        raw, value, cos, sin = source(h, block, lo)
        v_buf[to] = value
        (hat,) = norm_forward([raw], k_gain, cos, sin)
        k_hat[to] = hat
        k_turned[:, to] = jnp.transpose(hat)

    def key_hidden(h, block, step):
        to = pl.ds(aligned(block * rows + step * tile), tile)
        zeros = jnp.zeros((tile, head), jnp.bfloat16)
        v_buf[to] = zeros
        k_hat[to] = zeros
        k_turned[:, to] = jnp.zeros((head, tile), jnp.bfloat16)

    def key_backward(h, block, step):
        lo = aligned(step * tile)
        sel = pl.ds(aligned(block * rows + lo), tile)
        raw, _, cos, sin = source(h, block, lo)
        dk = dk_acc[sel] * score_scale
        turned = dk * cos - pltpu.roll(dk, half, 1) * sin
        (raw_grad,), gain_part = norm_backward([turned], [raw], k_gain)
        gain_acc[...] += gain_part
        back = back_refs[reach - block - 1]
        back[pl.ds(lo, tile), lanes_of(h)] = raw_grad.astype(jnp.bfloat16)
        back[pl.ds(lo, tile), lanes_of(count + h)] = dv_acc[sel].astype(jnp.bfloat16)

    def key_unused(h, block, step):
        lo = aligned(step * tile)
        for j in (h, count + h):
            back_refs[reach - block - 1][pl.ds(lo, tile), lanes_of(j)] = jnp.zeros((tile, head), jnp.bfloat16)

    def over_far_keys(h, used, unused):
        for block in range(reach):
            first = jnp.clip((start_row - block * rows) // tile, 0, tiles)
            lax.fori_loop(0, first, lambda step, _: unused(h, block, step), None)
            lax.fori_loop(first, tiles, lambda step, _: used(h, block, step), None)

    def heads_of(ref, h, here):
        return jnp.concatenate([ref[here, lanes_of((first_head + h) * group + g)] for g in range(group)], 0)

    def tile_step(h, n, begin, length, blocks):
        lo = aligned(n * tile)
        here = pl.ds(lo, tile)
        query = heads_of(q_hat, h, here)
        grad_out = heads_of(do_ref, h, here)
        query_pos = base + lo + lax.broadcasted_iota(jnp.int32, (1, tile), 1)
        lower = first_visible(query_pos, jnp.zeros_like(query_pos)) - (origin + begin)
        lower = jnp.concatenate([lower] * group, 1)
        upper = jnp.concatenate([query_pos - (origin + begin)] * group, 1)
        offset = lax.broadcasted_iota(jnp.int32, (STRIP, lanes), 0)
        whole = isinstance(blocks, int)

        def fold(values):
            return values.reshape(STRIP // 8, 8, lanes)

        def over_blocks(step, init):
            return step(0, init) if whole else lax.fori_loop(0, blocks, step, init)

        def place_of(i):
            return 0 if whole else aligned(i * length)

        def strip(first, at):
            return pl.ds(first + at, STRIP)

        def products(i, top):
            first = place_of(i)
            keys = pl.ds(aligned(begin + first), length)
            score_buf[pl.ds(first, length)] = dot(k_hat[keys], query, (1, 1))
            soft_grad_buf[pl.ds(first, length)] = dot(v_buf[keys], grad_out, (1, 1))
            for at in range(0, length, STRIP):
                visible = offset >= lower - (first + at)
                if not whole or at + STRIP > length - tile:
                    visible &= offset <= upper - (first + at)
                sel = strip(first, at)
                part = jnp.where(visible, score_buf[sel], masked_score)
                score_buf[sel] = part
                top = jnp.maximum(top, jnp.max(fold(part), axis=0))
            return top

        top = over_blocks(products, jnp.full((8, lanes), masked_score, jnp.float32))
        top = jnp.max(top, axis=0, keepdims=True) * exp_scale

        def weigh(i, sums):
            first = place_of(i)
            total, product = sums
            for at in range(0, length, STRIP):
                sel = strip(first, at)
                weight = jnp.exp2(score_buf[sel] * exp_scale - top)
                score_buf[sel] = weight
                total += jnp.sum(fold(weight), axis=0)
                product += jnp.sum(fold(weight * soft_grad_buf[sel]), axis=0)
            return total, product

        total, product = over_blocks(weigh, (jnp.zeros((8, lanes), jnp.float32),) * 2)
        recip = 1.0 / jnp.sum(total, axis=0, keepdims=True)
        delta = jnp.sum(product, axis=0, keepdims=True) * recip
        out = pl.ds(aligned(n * lanes), lanes)

        def finish(i, _):
            first = place_of(i)
            keys = pl.ds(aligned(begin + first), length)
            for at in range(0, length, STRIP):
                sel = strip(first, at)
                soft = score_buf[sel] * recip
                soft_buf[at : at + STRIP] = soft.astype(jnp.bfloat16)
                ds_buf[at : at + STRIP] = (soft * (soft_grad_buf[sel] - delta)).astype(jnp.bfloat16)
            dk_acc[keys] += dot(ds_buf[:length], query, (1, 0))
            dv_acc[keys] += dot(soft_buf[:length], grad_out, (1, 0))
            grad = dot(k_turned[:, keys], ds_buf[:length], (1, 0))
            if whole:
                dq_out[h, :, out] = grad
            else:
                dq_out[h, :, out] += grad
            return 0

        if not whole:
            dq_out[h, :, out] = jnp.zeros((head, lanes), jnp.float32)
        over_blocks(finish, 0)

    def query_tile(h, n):
        end = far_rows + (n + 1) * tile
        need = end - (first_visible(base + n * tile, 0) - origin)
        lengths = [k * TILE for k in (3, 4) if k * TILE <= far_rows + tile]
        for shorter, length in zip([0] + lengths, lengths):
            body = functools.partial(tile_step, h, n, aligned(end - length), length, 1)
            pl.when((need > shorter) & (need <= length))(body)
        count = (need + tile - 1) // tile
        body = functools.partial(tile_step, h, n, aligned(end - count * tile), tile, count)
        pl.when(need > max([0] + lengths))(body)

    mine = slice(far_rows, all_keys)

    def head_step(h, _):
        own = lanes_of(first_head + h)
        k_hat[mine] = k_own[:, own]
        v_buf[mine] = v_all[:, own]
        k_turned[:, mine] = k_own_turned[own]
        dk_acc[...] = jnp.zeros_like(dk_acc)
        dv_acc[...] = jnp.zeros_like(dv_acc)
        over_far_keys(h, key_forward, key_hidden)
        lax.fori_loop(0, tiles, lambda n, _: query_tile(h, n), None)
        over_far_keys(h, key_backward, key_unused)
        dk_out[:, lanes_of(h)] = dk_acc[mine]
        dv_out[:, lanes_of(h)] = dv_acc[mine]

    lax.fori_loop(0, count, head_step, None)
    gain_out[0, 0:1, :] = jnp.zeros((1, head), jnp.float32)
    gain_out[0, 1:2, :] = jnp.sum(gain_acc[...], axis=0, keepdims=True)


def attention(meta, gains, cos, sin, q_hat, k_hat, k_turned, do, v, far, first_head, count, docs):
    rows = q_hat.shape[0]
    head = gains.shape[1]
    group = q_hat.shape[1] // k_hat.shape[1]
    reach = len(far)
    operands = [meta, gains, cos, sin, q_hat, k_hat, k_turned, do, v, *far]
    keys = (reach + 1) * rows
    lanes = group * 2 * TILE
    out_shape = [jax.ShapeDtypeStruct((count, head, group * rows), jnp.float32)]
    out_shape += [jax.ShapeDtypeStruct((rows, count * head), jnp.float32)] * 2
    out_shape += [jax.ShapeDtypeStruct((rows, 2 * count * head), jnp.bfloat16)] * reach
    out_shape += [jax.ShapeDtypeStruct((1, 2, head), jnp.float32)]
    in_vmem = pl.BlockSpec(memory_space=pltpu.VMEM)
    return pl.pallas_call(
        functools.partial(attention_kernel, reach, docs, first_head, count),
        in_specs=[pl.BlockSpec(memory_space=pltpu.SMEM)] + [in_vmem] * (len(operands) - 1),
        out_specs=[in_vmem] * len(out_shape),
        scratch_shapes=[pltpu.VMEM((keys, lanes), jnp.float32)] * 2
        + [pltpu.VMEM((4 * TILE, lanes), jnp.bfloat16)] * 2
        + [pltpu.VMEM((keys, head), jnp.bfloat16)] * 2
        + [pltpu.VMEM((head, keys), jnp.bfloat16)]
        + [pltpu.VMEM((keys, head), jnp.float32)] * 2
        + [pltpu.VMEM((8, head), jnp.float32)],
        out_shape=out_shape,
        compiler_params=pltpu.CompilerParams(vmem_limit_bytes=24 * 1024 * 1024),
        cost_estimate=pl.CostEstimate(flops=1, bytes_accessed=1, transcendentals=0),
    )(*operands)


def backward_kernel(chained, first_head, parts, *refs):
    refs = refs[1 if chained else 0 :]
    gains_ref, cos_ref, sin_ref, turned_ref, q_ref, k_ref, dq_parts, dk_parts = refs[:8]
    part_refs = refs[8 : 8 + parts]
    dq_out, k_grads, gain_out, dq_buf, gain_acc, sem = refs[8 + parts :]
    count = dq_parts.shape[0]
    rows = q_ref.shape[0]
    head = gains_ref.shape[1]
    half = head // 2
    group = q_ref.shape[1] // k_ref.shape[1]
    gain_acc[...] = jnp.zeros_like(gain_acc)

    def query_step(n, _):
        lo = aligned(n * TILE)
        here = pl.ds(lo, TILE)
        cos, sin = turned_ref[:half, here], turned_ref[half:, here]
        for batch in in_batches(range(count * group), 4):
            turned = []
            for i in batch:
                at = (n // 2) * (2 * group * TILE) + (i % group) * 2 * TILE + (n % 2) * TILE
                grad = dq_parts[i // group, :, pl.ds(aligned(at), TILE)] * score_scale
                low, high = grad[:half], grad[half:]
                turned.append(jnp.concatenate([low * cos + high * sin, high * cos - low * sin], 0))
            turned = [jnp.transpose(t) for t in turned]
            raws = [q_ref[here, columns(first_head * group + i, head)] for i in batch]
            grads, gain_part = norm_backward(turned, raws, gains_ref[0:1, :])
            gain_acc[0:8] += gain_part
            for i, grad in zip(batch, grads):
                dq_buf[here, columns(i, head)] = grad.astype(jnp.bfloat16)

    def key_step(n, _):
        here = pl.ds(aligned(n * TILE), TILE)
        cos, sin = cos_ref[here], sin_ref[here]
        for batch in in_batches(range(count), 4):
            grads = [dk_parts[here, columns(j, head)] * score_scale for j in batch]
            turned = [dk * cos - pltpu.roll(dk, half, 1) * sin for dk in grads]
            raws = [k_ref[here, columns(first_head + j, head)] for j in batch]
            grads, gain_part = norm_backward(turned, raws, gains_ref[1:2, :])
            gain_acc[8:16] += gain_part
            for j, grad in zip(batch, grads):
                k_grads[here, columns(j, head)] = grad

    lax.fori_loop(0, rows // TILE, query_step, None)
    mine = dq_out.at[:, first_head * group * head : (first_head + count) * group * head]
    copy = pltpu.make_async_copy(dq_buf, mine, sem)
    copy.start()
    lax.fori_loop(0, rows // TILE, key_step, None)
    sums = [jnp.sum(gain_acc[at : at + 8], axis=0, keepdims=True) for at in (0, 8)]
    total = jnp.concatenate(sums, 0) + sum(ref[0] for ref in part_refs)
    gain_out[...] = jnp.broadcast_to(total[None], gain_out.shape)
    copy.wait()


def backward(gains, cos, sin, turned, q, k, dqs, dks, parts, carried, first_head, copies):
    count, head = dqs.shape[:2]
    group = q.shape[1] // k.shape[1]
    in_vmem = pl.BlockSpec(memory_space=pltpu.VMEM)
    operands = [gains, cos, sin, turned, q, k, dqs, dks, *parts]
    in_specs = [in_vmem] * len(operands)
    aliases = {}
    if carried is not None:
        operands.insert(0, carried)
        in_specs.insert(0, pl.BlockSpec(memory_space=pl.ANY))
        aliases = {0: 0}
    return pl.pallas_call(
        functools.partial(backward_kernel, carried is not None, first_head, len(parts)),
        in_specs=in_specs,
        out_specs=[pl.BlockSpec(memory_space=pl.ANY), in_vmem, in_vmem],
        scratch_shapes=[
            pltpu.VMEM((q.shape[0], count * group * head), jnp.bfloat16),
            pltpu.VMEM((16, head), jnp.float32),
            pltpu.SemaphoreType.DMA,
        ],
        out_shape=[
            jax.ShapeDtypeStruct(q.shape, jnp.bfloat16),
            jax.ShapeDtypeStruct(dks.shape, jnp.float32),
            jax.ShapeDtypeStruct((copies, *gains.shape), jnp.float32),
        ],
        input_output_aliases=aliases,
        compiler_params=pltpu.CompilerParams(vmem_limit_bytes=16 * 1024 * 1024),
        cost_estimate=pl.CostEstimate(flops=1, bytes_accessed=1, transcendentals=0),
    )(*operands)


def join_kernel(reach, own_key, own_value, *refs):
    width = own_key.shape[1]
    key_out, value_out = refs[-2:]
    key, value = own_key[...], own_value[...]
    for back in refs[:reach]:
        block = back[...].astype(jnp.float32)
        key = key + block[:, :width]
        value = value + block[:, width:]
    key_out[...] = key.astype(jnp.bfloat16)
    value_out[...] = value.astype(jnp.bfloat16)


def join(own_key, own_value, back, carried, place, like, cost):
    rows, width = own_key.shape
    reach = len(back)
    steps = 4
    operands = [own_key, own_value, *back]
    in_specs = [pl.BlockSpec((rows // steps, width), lambda i: (i, 0))] * 2
    in_specs += [pl.BlockSpec((rows // steps, 2 * width), lambda i: (i, 0))] * reach
    aliases = {}
    if carried is not None:
        aliases = {len(operands): 0, len(operands) + 1: 1}
        operands += carried
        in_specs += [pl.BlockSpec(memory_space=pl.ANY)] * 2
    return pl.pallas_call(
        functools.partial(join_kernel, reach),
        grid=(steps,),
        in_specs=in_specs,
        out_specs=[pl.BlockSpec((rows // steps, width), lambda i: (i, place))] * 2,
        out_shape=[jax.ShapeDtypeStruct(like.shape, like.dtype)] * 2,
        input_output_aliases=aliases,
        compiler_params=pltpu.CompilerParams(vmem_limit_bytes=8 * 1024 * 1024),
        cost_estimate=pl.CostEstimate(flops=1, bytes_accessed=cost, transcendentals=0),
    )(*operands)


def shards(
    query_raw, key_before_norm, value_input, out_cotangent, query_gain, key_norm_gain, doc_starts, windows
):
    rows = query_raw.shape[0]
    head = query_gain.shape[0]
    key_heads = key_before_norm.shape[1] // head
    shard_count = lax.axis_size("seq")
    slab_shards = shard_count // SLABS
    slab_length = slab_shards * rows
    shift = slab_length // 2 // rows
    assert slab_shards * SLABS == shard_count and shift * rows * 2 == slab_length
    reach = min((WINDOW - 1) // rows + 1, slab_shards - 1)
    docs = doc_starts.shape[1]

    def links(distance):
        found = []
        for i in range(shard_count):
            if (i - shift) % slab_shards + distance < slab_shards:
                found.append((i, (i + distance) % shard_count))
        return found

    placed = (lax.axis_index("seq") - shift) % shard_count
    slab = placed // slab_shards
    base = (placed % slab_shards) * rows
    starts = lax.dynamic_index_in_dim(doc_starts, slab, 0, keepdims=False)
    window = lax.dynamic_index_in_dim(windows, slab, 0, keepdims=True)
    meta = jnp.concatenate([base[None], window, starts]).astype(jnp.int32)
    positions = jnp.concatenate(
        [base - d * rows + jnp.arange(rows, dtype=jnp.int32) for d in range(reach + 1)]
    )
    begins = jnp.max(jnp.where(starts[None, :] <= positions[:, None], starts[None, :], 0), axis=1)
    spacing = jnp.arange(head // 2, dtype=jnp.float32) * (2.0 / head)
    angle = (positions - begins).astype(jnp.float32)[:, None] * (10000.0 ** (-spacing))[None, :]
    cosine, sine = jnp.cos(angle), jnp.sin(angle)
    count = 2 if key_heads % 2 == 0 else 1
    groups = range(0, key_heads, count)
    far = []
    sent = (key_before_norm, value_input)
    for j in groups:
        packed = jnp.concatenate([a[:, j * head : (j + count) * head] for a in sent], 1)
        far.append([lax.ppermute(packed, "seq", links(d)) for d in range(1, reach + 1)])
        if j == 0:
            *sent, cosine, sine = lax.optimization_barrier((*sent, cosine, sine))
    cos_table = jnp.concatenate([cosine, cosine], axis=1)
    sin_table = jnp.concatenate([-sine, sine], axis=1)
    across = (10000.0 ** (-spacing))[:, None] * (positions - begins)[:rows].astype(jnp.float32)[None, :]
    turned = jnp.concatenate([jnp.cos(across), jnp.sin(across)], axis=0)
    gains = jnp.stack([query_gain, key_norm_gain])

    q_hat, k_hat, k_turned = prepare(gains, cos_table, sin_table, query_raw, key_before_norm)
    query_gradient, everyone = None, None
    owns, backs = [], []
    for j, blocks in zip(groups, far):
        dqs, dks, value_own, *back, part = attention(
            meta, gains, cos_table, sin_table, q_hat, k_hat, k_turned, out_cotangent, value_input, blocks, j, count, docs
        )
        backs.append([lax.ppermute(b, "seq", [(to, at) for at, to in links(d)]) for d, b in enumerate(back, 1)])
        last = j + count == key_heads
        query_gradient, key_own, everyone = backward(
            gains, cos_table, sin_table, turned, query_raw, key_before_norm, dqs, dks,
            [part] if everyone is None else [part, everyone], query_gradient, j,
            shard_count * lax.axis_size("head") if last else 1,
        )
        owns.append((key_own, value_own))
        if not last:
            meta, everyone = lax.optimization_barrier((meta, everyone))
    if len(backs) > 1:
        everyone, backs[:-1] = lax.optimization_barrier((everyone, backs[:-1]))
    gathered = lax.all_to_all(everyone, ("seq", "head"), 0, 0)
    carried = None
    for n, (own, back) in enumerate(zip(owns, backs)):
        carried = join(*own, back, carried, n, key_before_norm, 1 if n + 1 < len(owns) else 200 * 10**6)
    total = jnp.sum(gathered, axis=0)
    return query_gradient, *carried, total[0], total[1]


def solution(mesh):
    placed = (P("seq", "head"),) * 4 + (P(),) * 4
    return jax.shard_map(
        shards,
        mesh=mesh,
        in_specs=placed,
        out_specs=(P("seq", "head"), P("seq", "head"), P("seq", "head"), P(), P()),
        check_vma=False,
    )
```

```python
import functools

import jax
import jax.numpy as jnp
from jax import lax
from jax.experimental import pallas as pl
from jax.experimental.pallas import tpu as pltpu
from jax.sharding import PartitionSpec as P

WINDOW = 1024
SLABS = 4

score_scale = 168.0 ** (-0.5)
log2_e = 1.4426950408889634
norm_eps = 1e-06
masked_score = -1e30
exp_scale = score_scale * log2_e

TILE = 128
STRIP = 32


def dot(a, b, contract):
    return lax.dot_general(a, b, ((contract[:1], contract[1:]), ((), ())), preferred_element_type=jnp.float32)


def inverse_rms(floats):
    return lax.rsqrt(jnp.mean(floats * floats, axis=-1, keepdims=True) + norm_eps)


def norm_forward(raws, gain, cosine, sine):
    floats = [raw.astype(jnp.float32) for raw in raws]
    inverses = [inverse_rms(f) for f in floats]
    scaled = [f * i * gain for f, i in zip(floats, inverses)]
    rolled = [pltpu.roll(s, s.shape[1] // 2, 1) for s in scaled]
    return [(s * cosine + r * sine).astype(jnp.bfloat16) for s, r in zip(scaled, rolled)]


def norm_backward(turned, raws, gain):
    floats = [raw.astype(jnp.float32) for raw in raws]
    inverses = [inverse_rms(f) for f in floats]
    weighted = [t * gain for t in turned]
    corrections = [jnp.mean(w * f, axis=-1, keepdims=True) for w, f in zip(weighted, floats)]
    gain_grad = sum(
        jnp.sum((t * (f * i)).reshape(-1, 8, t.shape[1]), axis=0) for t, f, i in zip(turned, floats, inverses)
    )
    grads = [
        i * w - f * (i * i * i * c) for f, i, w, c in zip(floats, inverses, weighted, corrections)
    ]
    return grads, gain_grad


def aligned(value):
    return pl.multiple_of(value, TILE)


def in_batches(items, size):
    return [items[n : n + size] for n in range(0, len(items), size)]


def columns(j, head):
    return slice(j * head, (j + 1) * head)


def prepare_kernel(gains_ref, cos_ref, sin_ref, q_ref, k_ref, q_hat, k_hat, k_turned):
    rows = q_ref.shape[0]
    head = gains_ref.shape[1]

    def step(n, _):
        here = pl.ds(aligned(n * TILE), TILE)
        cos, sin = cos_ref[here], sin_ref[here]
        for raw, row, out in ((q_ref, 0, q_hat), (k_ref, 1, k_hat)):
            for batch in in_batches(range(raw.shape[1] // head), 4):
                hats = norm_forward([raw[here, columns(j, head)] for j in batch], gains_ref[row : row + 1], cos, sin)
                for j, hat in zip(batch, hats):
                    out[here, columns(j, head)] = hat
                    if row == 1:
                        k_turned[columns(j, head), here] = jnp.transpose(hat)

    lax.fori_loop(0, rows // TILE, step, None)


def prepare(gains, cos, sin, q, k):
    in_vmem = pl.BlockSpec(memory_space=pltpu.VMEM)
    return pl.pallas_call(
        prepare_kernel,
        in_specs=[in_vmem] * 5,
        out_specs=[in_vmem] * 3,
        out_shape=[jax.ShapeDtypeStruct(shape, jnp.bfloat16) for shape in (q.shape, k.shape, k.shape[::-1])],
        compiler_params=pltpu.CompilerParams(vmem_limit_bytes=16 * 1024 * 1024),
        cost_estimate=pl.CostEstimate(flops=1, bytes_accessed=1, transcendentals=0),
    )(gains, cos, sin, q, k)


def attention_kernel(reach, docs, first_head, count, meta, *refs):
    gains_ref, cos_ref, sin_ref, q_hat, k_own, k_own_turned, do_ref, v_all = refs[:8]
    far_refs = refs[8 : 8 + reach]
    refs = refs[8 + reach :]
    dq_out, dk_out, dv_out = refs[:3]
    back_refs = refs[3 : 3 + reach]
    gain_out = refs[3 + reach]
    score_buf, soft_grad_buf, soft_buf, ds_buf, k_hat, v_buf, k_turned, dk_acc, dv_acc, gain_acc = refs[4 + reach :]
    rows = q_hat.shape[0]
    head = gains_ref.shape[1]
    half = head // 2
    group = q_hat.shape[1] // k_own.shape[1]
    tile = 2 * TILE
    lanes = group * tile
    tiles = rows // tile
    far_rows = reach * rows
    all_keys = far_rows + rows
    base, window = meta[0], meta[1]
    origin = base - far_rows
    k_gain = gains_ref[1:2, :]
    gain_acc[...] = jnp.zeros_like(gain_acc)

    def first_visible(position, zero):
        first = zero
        for j in range(docs):
            start = meta[2 + j]
            first = jnp.maximum(first, jnp.where(position >= start, start, 0))
        return jnp.maximum(first, position - window + 1)

    start_row = first_visible(base, 0) - origin

    def lanes_of(j):
        return pl.ds(aligned(j * head), head)

    def source(h, block, lo):
        far = far_refs[reach - block - 1]
        at = pl.ds(lo, tile)
        table = pl.ds(aligned((reach - block) * rows + lo), tile)
        return far[at, lanes_of(h)], far[at, lanes_of(count + h)], cos_ref[table], sin_ref[table]

    def key_forward(h, block, step):
        lo = aligned(step * tile)
        to = pl.ds(aligned(block * rows + lo), tile)
        raw, value, cos, sin = source(h, block, lo)
        v_buf[to] = value
        (hat,) = norm_forward([raw], k_gain, cos, sin)
        k_hat[to] = hat
        k_turned[:, to] = jnp.transpose(hat)

    def key_hidden(h, block, step):
        to = pl.ds(aligned(block * rows + step * tile), tile)
        zeros = jnp.zeros((tile, head), jnp.bfloat16)
        v_buf[to] = zeros
        k_hat[to] = zeros
        k_turned[:, to] = jnp.zeros((head, tile), jnp.bfloat16)

    def key_backward(h, block, step):
        lo = aligned(step * tile)
        sel = pl.ds(aligned(block * rows + lo), tile)
        raw, _, cos, sin = source(h, block, lo)
        dk = dk_acc[sel] * score_scale
        turned = dk * cos - pltpu.roll(dk, half, 1) * sin
        (raw_grad,), gain_part = norm_backward([turned], [raw], k_gain)
        gain_acc[...] += gain_part
        back = back_refs[reach - block - 1]
        back[pl.ds(lo, tile), lanes_of(h)] = raw_grad.astype(jnp.bfloat16)
        back[pl.ds(lo, tile), lanes_of(count + h)] = dv_acc[sel].astype(jnp.bfloat16)

    def key_unused(h, block, step):
        lo = aligned(step * tile)
        for j in (h, count + h):
            back_refs[reach - block - 1][pl.ds(lo, tile), lanes_of(j)] = jnp.zeros((tile, head), jnp.bfloat16)

    def over_far_keys(h, used, unused):
        for block in range(reach):
            first = jnp.clip((start_row - block * rows) // tile, 0, tiles)
            lax.fori_loop(0, first, lambda step, _: unused(h, block, step), None)
            lax.fori_loop(first, tiles, lambda step, _: used(h, block, step), None)

    def heads_of(ref, h, here):
        return jnp.concatenate([ref[here, lanes_of((first_head + h) * group + g)] for g in range(group)], 0)

    def tile_step(h, n, begin, length, blocks):
        lo = aligned(n * tile)
        here = pl.ds(lo, tile)
        query = heads_of(q_hat, h, here)
        grad_out = heads_of(do_ref, h, here)
        query_pos = base + lo + lax.broadcasted_iota(jnp.int32, (1, tile), 1)
        lower = first_visible(query_pos, jnp.zeros_like(query_pos)) - (origin + begin)
        lower = jnp.concatenate([lower] * group, 1)
        upper = jnp.concatenate([query_pos - (origin + begin)] * group, 1)
        offset = lax.broadcasted_iota(jnp.int32, (STRIP, lanes), 0)
        whole = isinstance(blocks, int)

        def fold(values):
            return values.reshape(STRIP // 8, 8, lanes)

        def over_blocks(step, init):
            return step(0, init) if whole else lax.fori_loop(0, blocks, step, init)

        def place_of(i):
            return 0 if whole else aligned(i * length)

        def strip(first, at):
            return pl.ds(first + at, STRIP)

        def products(i, top):
            first = place_of(i)
            keys = pl.ds(aligned(begin + first), length)
            score_buf[pl.ds(first, length)] = dot(k_hat[keys], query, (1, 1))
            soft_grad_buf[pl.ds(first, length)] = dot(v_buf[keys], grad_out, (1, 1))
            for at in range(0, length, STRIP):
                visible = offset >= lower - (first + at)
                if not whole or at + STRIP > length - tile:
                    visible &= offset <= upper - (first + at)
                sel = strip(first, at)
                part = jnp.where(visible, score_buf[sel], masked_score)
                score_buf[sel] = part
                top = jnp.maximum(top, jnp.max(fold(part), axis=0))
            return top

        top = over_blocks(products, jnp.full((8, lanes), masked_score, jnp.float32))
        top = jnp.max(top, axis=0, keepdims=True) * exp_scale

        def weigh(i, sums):
            first = place_of(i)
            total, product = sums
            for at in range(0, length, STRIP):
                sel = strip(first, at)
                weight = jnp.exp2(score_buf[sel] * exp_scale - top)
                score_buf[sel] = weight
                total += jnp.sum(fold(weight), axis=0)
                product += jnp.sum(fold(weight * soft_grad_buf[sel]), axis=0)
            return total, product

        total, product = over_blocks(weigh, (jnp.zeros((8, lanes), jnp.float32),) * 2)
        recip = 1.0 / jnp.sum(total, axis=0, keepdims=True)
        delta = jnp.sum(product, axis=0, keepdims=True) * recip
        out = pl.ds(aligned(n * lanes), lanes)

        def finish(i, _):
            first = place_of(i)
            keys = pl.ds(aligned(begin + first), length)
            for at in range(0, length, STRIP):
                sel = strip(first, at)
                soft = score_buf[sel] * recip
                soft_buf[at : at + STRIP] = soft.astype(jnp.bfloat16)
                ds_buf[at : at + STRIP] = (soft * (soft_grad_buf[sel] - delta)).astype(jnp.bfloat16)
            dk_acc[keys] += dot(ds_buf[:length], query, (1, 0))
            dv_acc[keys] += dot(soft_buf[:length], grad_out, (1, 0))
            grad = dot(k_turned[:, keys], ds_buf[:length], (1, 0))
            if whole:
                dq_out[h, :, out] = grad
            else:
                dq_out[h, :, out] += grad
            return 0

        if not whole:
            dq_out[h, :, out] = jnp.zeros((head, lanes), jnp.float32)
        over_blocks(finish, 0)

    def query_tile(h, n):
        end = far_rows + (n + 1) * tile
        need = end - (first_visible(base + n * tile, 0) - origin)
        lengths = [k * TILE for k in (3, 4, 6) if k * TILE <= far_rows + tile]
        for shorter, length in zip([0] + lengths, lengths):
            body = functools.partial(tile_step, h, n, aligned(end - length), length, 1)
            pl.when((need > shorter) & (need <= length))(body)
        count = (need + tile - 1) // tile
        body = functools.partial(tile_step, h, n, aligned(end - count * tile), tile, count)
        pl.when(need > max([0] + lengths))(body)

    mine = slice(far_rows, all_keys)

    def head_step(h, _):
        own = lanes_of(first_head + h)
        k_hat[mine] = k_own[:, own]
        v_buf[mine] = v_all[:, own]
        k_turned[:, mine] = k_own_turned[own]
        dk_acc[...] = jnp.zeros_like(dk_acc)
        dv_acc[...] = jnp.zeros_like(dv_acc)
        over_far_keys(h, key_forward, key_hidden)
        lax.fori_loop(0, tiles, lambda n, _: query_tile(h, n), None)
        over_far_keys(h, key_backward, key_unused)
        dk_out[:, lanes_of(h)] = dk_acc[mine]
        dv_out[:, lanes_of(h)] = dv_acc[mine]

    lax.fori_loop(0, count, head_step, None)
    gain_out[0, 0:1, :] = jnp.zeros((1, head), jnp.float32)
    gain_out[0, 1:2, :] = jnp.sum(gain_acc[...], axis=0, keepdims=True)


def attention(meta, gains, cos, sin, q_hat, k_hat, k_turned, do, v, far, first_head, count, docs):
    rows = q_hat.shape[0]
    head = gains.shape[1]
    group = q_hat.shape[1] // k_hat.shape[1]
    reach = len(far)
    operands = [meta, gains, cos, sin, q_hat, k_hat, k_turned, do, v, *far]
    keys = (reach + 1) * rows
    lanes = group * 2 * TILE
    out_shape = [jax.ShapeDtypeStruct((count, head, group * rows), jnp.float32)]
    out_shape += [jax.ShapeDtypeStruct((rows, count * head), jnp.float32)] * 2
    out_shape += [jax.ShapeDtypeStruct((rows, 2 * count * head), jnp.bfloat16)] * reach
    out_shape += [jax.ShapeDtypeStruct((1, 2, head), jnp.float32)]
    in_vmem = pl.BlockSpec(memory_space=pltpu.VMEM)
    return pl.pallas_call(
        functools.partial(attention_kernel, reach, docs, first_head, count),
        in_specs=[pl.BlockSpec(memory_space=pltpu.SMEM)] + [in_vmem] * (len(operands) - 1),
        out_specs=[in_vmem] * len(out_shape),
        scratch_shapes=[pltpu.VMEM((keys, lanes), jnp.float32)] * 2
        + [pltpu.VMEM((6 * TILE, lanes), jnp.bfloat16)] * 2
        + [pltpu.VMEM((keys, head), jnp.bfloat16)] * 2
        + [pltpu.VMEM((head, keys), jnp.bfloat16)]
        + [pltpu.VMEM((keys, head), jnp.float32)] * 2
        + [pltpu.VMEM((8, head), jnp.float32)],
        out_shape=out_shape,
        compiler_params=pltpu.CompilerParams(vmem_limit_bytes=24 * 1024 * 1024),
        cost_estimate=pl.CostEstimate(flops=1, bytes_accessed=1, transcendentals=0),
    )(*operands)


def backward_kernel(chained, first_head, parts, *refs):
    refs = refs[1 if chained else 0 :]
    gains_ref, cos_ref, sin_ref, turned_ref, q_ref, k_ref, dq_parts, dk_parts = refs[:8]
    part_refs = refs[8 : 8 + parts]
    dq_out, k_grads, gain_out, dq_buf, gain_acc, sem = refs[8 + parts :]
    count = dq_parts.shape[0]
    rows = q_ref.shape[0]
    head = gains_ref.shape[1]
    half = head // 2
    group = q_ref.shape[1] // k_ref.shape[1]
    gain_acc[...] = jnp.zeros_like(gain_acc)

    def query_step(n, _):
        lo = aligned(n * TILE)
        here = pl.ds(lo, TILE)
        cos, sin = turned_ref[:half, here], turned_ref[half:, here]
        for batch in in_batches(range(count * group), 4):
            turned = []
            for i in batch:
                at = (n // 2) * (2 * group * TILE) + (i % group) * 2 * TILE + (n % 2) * TILE
                grad = dq_parts[i // group, :, pl.ds(aligned(at), TILE)] * score_scale
                low, high = grad[:half], grad[half:]
                turned.append(jnp.concatenate([low * cos + high * sin, high * cos - low * sin], 0))
            turned = [jnp.transpose(t) for t in turned]
            raws = [q_ref[here, columns(first_head * group + i, head)] for i in batch]
            grads, gain_part = norm_backward(turned, raws, gains_ref[0:1, :])
            gain_acc[0:8] += gain_part
            for i, grad in zip(batch, grads):
                dq_buf[here, columns(i, head)] = grad.astype(jnp.bfloat16)

    def key_step(n, _):
        here = pl.ds(aligned(n * TILE), TILE)
        cos, sin = cos_ref[here], sin_ref[here]
        for batch in in_batches(range(count), 4):
            grads = [dk_parts[here, columns(j, head)] * score_scale for j in batch]
            turned = [dk * cos - pltpu.roll(dk, half, 1) * sin for dk in grads]
            raws = [k_ref[here, columns(first_head + j, head)] for j in batch]
            grads, gain_part = norm_backward(turned, raws, gains_ref[1:2, :])
            gain_acc[8:16] += gain_part
            for j, grad in zip(batch, grads):
                k_grads[here, columns(j, head)] = grad

    lax.fori_loop(0, rows // TILE, query_step, None)
    mine = dq_out.at[:, first_head * group * head : (first_head + count) * group * head]
    copy = pltpu.make_async_copy(dq_buf, mine, sem)
    copy.start()
    lax.fori_loop(0, rows // TILE, key_step, None)
    sums = [jnp.sum(gain_acc[at : at + 8], axis=0, keepdims=True) for at in (0, 8)]
    total = jnp.concatenate(sums, 0) + sum(ref[0] for ref in part_refs)
    gain_out[...] = jnp.broadcast_to(total[None], gain_out.shape)
    copy.wait()


def backward(gains, cos, sin, turned, q, k, dqs, dks, parts, carried, first_head, copies):
    count, head = dqs.shape[:2]
    group = q.shape[1] // k.shape[1]
    in_vmem = pl.BlockSpec(memory_space=pltpu.VMEM)
    operands = [gains, cos, sin, turned, q, k, dqs, dks, *parts]
    in_specs = [in_vmem] * len(operands)
    aliases = {}
    if carried is not None:
        operands.insert(0, carried)
        in_specs.insert(0, pl.BlockSpec(memory_space=pl.ANY))
        aliases = {0: 0}
    return pl.pallas_call(
        functools.partial(backward_kernel, carried is not None, first_head, len(parts)),
        in_specs=in_specs,
        out_specs=[pl.BlockSpec(memory_space=pl.ANY), in_vmem, in_vmem],
        scratch_shapes=[
            pltpu.VMEM((q.shape[0], count * group * head), jnp.bfloat16),
            pltpu.VMEM((16, head), jnp.float32),
            pltpu.SemaphoreType.DMA,
        ],
        out_shape=[
            jax.ShapeDtypeStruct(q.shape, jnp.bfloat16),
            jax.ShapeDtypeStruct(dks.shape, jnp.float32),
            jax.ShapeDtypeStruct((copies, *gains.shape), jnp.float32),
        ],
        input_output_aliases=aliases,
        compiler_params=pltpu.CompilerParams(vmem_limit_bytes=16 * 1024 * 1024),
        cost_estimate=pl.CostEstimate(flops=1, bytes_accessed=1, transcendentals=0),
    )(*operands)


def join_kernel(reach, own_key, own_value, *refs):
    width = own_key.shape[1]
    key_out, value_out = refs[-2:]
    key, value = own_key[...], own_value[...]
    for back in refs[:reach]:
        block = back[...].astype(jnp.float32)
        key = key + block[:, :width]
        value = value + block[:, width:]
    key_out[...] = key.astype(jnp.bfloat16)
    value_out[...] = value.astype(jnp.bfloat16)


def join(own_key, own_value, back, carried, place, like, cost):
    rows, width = own_key.shape
    reach = len(back)
    steps = 4
    operands = [own_key, own_value, *back]
    in_specs = [pl.BlockSpec((rows // steps, width), lambda i: (i, 0))] * 2
    in_specs += [pl.BlockSpec((rows // steps, 2 * width), lambda i: (i, 0))] * reach
    aliases = {}
    if carried is not None:
        aliases = {len(operands): 0, len(operands) + 1: 1}
        operands += carried
        in_specs += [pl.BlockSpec(memory_space=pl.ANY)] * 2
    return pl.pallas_call(
        functools.partial(join_kernel, reach),
        grid=(steps,),
        in_specs=in_specs,
        out_specs=[pl.BlockSpec((rows // steps, width), lambda i: (i, place))] * 2,
        out_shape=[jax.ShapeDtypeStruct(like.shape, like.dtype)] * 2,
        input_output_aliases=aliases,
        compiler_params=pltpu.CompilerParams(vmem_limit_bytes=8 * 1024 * 1024),
        cost_estimate=pl.CostEstimate(flops=1, bytes_accessed=cost, transcendentals=0),
    )(*operands)


def shards(
    query_raw, key_before_norm, value_input, out_cotangent, query_gain, key_norm_gain, doc_starts, windows
):
    rows = query_raw.shape[0]
    head = query_gain.shape[0]
    key_heads = key_before_norm.shape[1] // head
    shard_count = lax.axis_size("seq")
    slab_shards = shard_count // SLABS
    slab_length = slab_shards * rows
    shift = slab_length // 2 // rows
    assert slab_shards * SLABS == shard_count and shift * rows * 2 == slab_length
    reach = min((WINDOW - 1) // rows + 1, slab_shards - 1)
    docs = doc_starts.shape[1]

    def links(distance):
        found = []
        for i in range(shard_count):
            if (i - shift) % slab_shards + distance < slab_shards:
                found.append((i, (i + distance) % shard_count))
        return found

    placed = (lax.axis_index("seq") - shift) % shard_count
    slab = placed // slab_shards
    base = (placed % slab_shards) * rows
    starts = lax.dynamic_index_in_dim(doc_starts, slab, 0, keepdims=False)
    window = lax.dynamic_index_in_dim(windows, slab, 0, keepdims=True)
    meta = jnp.concatenate([base[None], window, starts]).astype(jnp.int32)
    positions = jnp.concatenate(
        [base - d * rows + jnp.arange(rows, dtype=jnp.int32) for d in range(reach + 1)]
    )
    begins = jnp.max(jnp.where(starts[None, :] <= positions[:, None], starts[None, :], 0), axis=1)
    spacing = jnp.arange(head // 2, dtype=jnp.float32) * (2.0 / head)
    angle = (positions - begins).astype(jnp.float32)[:, None] * (10000.0 ** (-spacing))[None, :]
    cosine, sine = jnp.cos(angle), jnp.sin(angle)
    count = 2 if key_heads % 2 == 0 else 1
    groups = range(0, key_heads, count)
    far = []
    sent = (key_before_norm, value_input)
    for j in groups:
        packed = jnp.concatenate([a[:, j * head : (j + count) * head] for a in sent], 1)
        far.append([lax.ppermute(packed, "seq", links(d)) for d in range(1, reach + 1)])
        if j == 0:
            *sent, cosine, sine = lax.optimization_barrier((*sent, cosine, sine))
    cos_table = jnp.concatenate([cosine, cosine], axis=1)
    sin_table = jnp.concatenate([-sine, sine], axis=1)
    across = (10000.0 ** (-spacing))[:, None] * (positions - begins)[:rows].astype(jnp.float32)[None, :]
    turned = jnp.concatenate([jnp.cos(across), jnp.sin(across)], axis=0)
    gains = jnp.stack([query_gain, key_norm_gain])

    q_hat, k_hat, k_turned = prepare(gains, cos_table, sin_table, query_raw, key_before_norm)
    query_gradient, everyone = None, None
    owns, backs = [], []
    for j, blocks in zip(groups, far):
        dqs, dks, value_own, *back, part = attention(
            meta, gains, cos_table, sin_table, q_hat, k_hat, k_turned, out_cotangent, value_input, blocks, j, count, docs
        )
        backs.append([lax.ppermute(b, "seq", [(to, at) for at, to in links(d)]) for d, b in enumerate(back, 1)])
        last = j + count == key_heads
        query_gradient, key_own, everyone = backward(
            gains, cos_table, sin_table, turned, query_raw, key_before_norm, dqs, dks,
            [part] if everyone is None else [part, everyone], query_gradient, j,
            shard_count * lax.axis_size("head") if last else 1,
        )
        owns.append((key_own, value_own))
        if not last:
            meta, everyone = lax.optimization_barrier((meta, everyone))
    if len(backs) > 1:
        everyone, backs[:-1] = lax.optimization_barrier((everyone, backs[:-1]))
    gathered = lax.all_to_all(everyone, ("seq", "head"), 0, 0)
    carried = None
    for n, (own, back) in enumerate(zip(owns, backs)):
        carried = join(*own, back, carried, n, key_before_norm, 1 if n + 1 < len(owns) else 200 * 10**6)
    total = jnp.sum(gathered, axis=0)
    return query_gradient, *carried, total[0], total[1]


def solution(mesh):
    placed = (P("seq", "head"),) * 4 + (P(),) * 4
    return jax.shard_map(
        shards,
        mesh=mesh,
        in_specs=placed,
        out_specs=(P("seq", "head"), P("seq", "head"), P("seq", "head"), P(), P()),
        check_vma=False,
    )
```

```python
import functools

import jax
import jax.numpy as jnp
from jax import lax
from jax.experimental import pallas as pl
from jax.experimental.pallas import tpu as pltpu
from jax.sharding import PartitionSpec as P

WINDOW = 1024
SLABS = 4

score_scale = 168.0 ** (-0.5)
log2_e = 1.4426950408889634
norm_eps = 1e-06
masked_score = -1e30
exp_scale = score_scale * log2_e

TILE = 128
STRIP = 32


def dot(a, b, contract):
    return lax.dot_general(a, b, ((contract[:1], contract[1:]), ((), ())), preferred_element_type=jnp.float32)


def inverse_rms(floats):
    return lax.rsqrt(jnp.mean(floats * floats, axis=-1, keepdims=True) + norm_eps)


def norm_forward(raws, gain, cosine, sine):
    floats = [raw.astype(jnp.float32) for raw in raws]
    inverses = [inverse_rms(f) for f in floats]
    scaled = [f * i * gain for f, i in zip(floats, inverses)]
    rolled = [pltpu.roll(s, s.shape[1] // 2, 1) for s in scaled]
    return [(s * cosine + r * sine).astype(jnp.bfloat16) for s, r in zip(scaled, rolled)]


def norm_backward(turned, raws, gain):
    floats = [raw.astype(jnp.float32) for raw in raws]
    inverses = [inverse_rms(f) for f in floats]
    weighted = [t * gain for t in turned]
    corrections = [jnp.mean(w * f, axis=-1, keepdims=True) for w, f in zip(weighted, floats)]
    gain_grad = sum(
        jnp.sum((t * (f * i)).reshape(-1, 8, t.shape[1]), axis=0) for t, f, i in zip(turned, floats, inverses)
    )
    grads = [
        i * w - f * (i * i * i * c) for f, i, w, c in zip(floats, inverses, weighted, corrections)
    ]
    return grads, gain_grad


def aligned(value):
    return pl.multiple_of(value, TILE)


def in_batches(items, size):
    return [items[n : n + size] for n in range(0, len(items), size)]


def columns(j, head):
    return slice(j * head, (j + 1) * head)


def prepare_kernel(gains_ref, cos_ref, sin_ref, q_ref, k_ref, q_hat, k_hat, k_turned):
    rows = q_ref.shape[0]
    head = gains_ref.shape[1]

    def step(n, _):
        here = pl.ds(aligned(n * TILE), TILE)
        cos, sin = cos_ref[here], sin_ref[here]
        for raw, row, out in ((q_ref, 0, q_hat), (k_ref, 1, k_hat)):
            for batch in in_batches(range(raw.shape[1] // head), 4):
                hats = norm_forward([raw[here, columns(j, head)] for j in batch], gains_ref[row : row + 1], cos, sin)
                for j, hat in zip(batch, hats):
                    out[here, columns(j, head)] = hat
                    if row == 1:
                        k_turned[columns(j, head), here] = jnp.transpose(hat)

    lax.fori_loop(0, rows // TILE, step, None)


def prepare(gains, cos, sin, q, k):
    in_vmem = pl.BlockSpec(memory_space=pltpu.VMEM)
    return pl.pallas_call(
        prepare_kernel,
        in_specs=[in_vmem] * 5,
        out_specs=[in_vmem] * 3,
        out_shape=[jax.ShapeDtypeStruct(shape, jnp.bfloat16) for shape in (q.shape, k.shape, k.shape[::-1])],
        compiler_params=pltpu.CompilerParams(vmem_limit_bytes=16 * 1024 * 1024),
        cost_estimate=pl.CostEstimate(flops=1, bytes_accessed=1, transcendentals=0),
    )(gains, cos, sin, q, k)


def attention_kernel(reach, docs, first_head, count, meta, *refs):
    gains_ref, cos_ref, sin_ref, q_hat, k_own, k_own_turned, do_ref, v_all = refs[:8]
    far_refs = refs[8 : 8 + reach]
    refs = refs[8 + reach :]
    dq_out, dk_out, dv_out = refs[:3]
    back_refs = refs[3 : 3 + reach]
    gain_out = refs[3 + reach]
    score_buf, soft_grad_buf, soft_buf, ds_buf, k_hat, v_buf, k_turned, dk_acc, dv_acc, gain_acc = refs[4 + reach :]
    rows = q_hat.shape[0]
    head = gains_ref.shape[1]
    half = head // 2
    group = q_hat.shape[1] // k_own.shape[1]
    tile = 2 * TILE
    lanes = group * tile
    tiles = rows // tile
    far_rows = reach * rows
    all_keys = far_rows + rows
    base, window = meta[0], meta[1]
    origin = base - far_rows
    k_gain = gains_ref[1:2, :]
    gain_acc[...] = jnp.zeros_like(gain_acc)

    def first_visible(position, zero):
        first = zero
        for j in range(docs):
            start = meta[2 + j]
            first = jnp.maximum(first, jnp.where(position >= start, start, 0))
        return jnp.maximum(first, position - window + 1)

    start_row = first_visible(base, 0) - origin

    def lanes_of(j):
        return pl.ds(aligned(j * head), head)

    def source(block, lo):
        far = far_refs[reach - block - 1]
        at = pl.ds(lo, tile)
        table = pl.ds(aligned((reach - block) * rows + lo), tile)
        raws = [far[at, columns(h, head)] for h in range(count)]
        values = [far[at, columns(count + h, head)] for h in range(count)]
        return raws, values, cos_ref[table], sin_ref[table]

    def key_forward(block, step):
        lo = aligned(step * tile)
        to = pl.ds(aligned(block * rows + lo), tile)
        raws, values, cos, sin = source(block, lo)
        hats = norm_forward(raws, k_gain, cos, sin)
        for h, (hat, value) in enumerate(zip(hats, values)):
            v_buf[h, to] = value
            k_hat[h, to] = hat
            k_turned[h, :, to] = jnp.transpose(hat)

    def key_hidden(block, step):
        to = pl.ds(aligned(block * rows + step * tile), tile)
        zeros = jnp.zeros((tile, head), jnp.bfloat16)
        for h in range(count):
            v_buf[h, to] = zeros
            k_hat[h, to] = zeros
            k_turned[h, :, to] = jnp.zeros((head, tile), jnp.bfloat16)

    def key_backward(block, step):
        lo = aligned(step * tile)
        sel = pl.ds(aligned(block * rows + lo), tile)
        raws, _, cos, sin = source(block, lo)
        grads = [dk_acc[h, sel] * score_scale for h in range(count)]
        turned = [dk * cos - pltpu.roll(dk, half, 1) * sin for dk in grads]
        grads, gain_part = norm_backward(turned, raws, k_gain)
        gain_acc[...] += gain_part
        back = back_refs[reach - block - 1]
        for h, grad in enumerate(grads):
            back[pl.ds(lo, tile), columns(h, head)] = grad.astype(jnp.bfloat16)
            back[pl.ds(lo, tile), columns(count + h, head)] = dv_acc[h, sel].astype(jnp.bfloat16)

    def key_unused(block, step):
        lo = aligned(step * tile)
        back_refs[reach - block - 1][pl.ds(lo, tile)] = jnp.zeros((tile, 2 * count * head), jnp.bfloat16)

    def over_far_keys(used, unused):
        for block in range(reach):
            first = jnp.clip((start_row - block * rows) // tile, 0, tiles)
            lax.fori_loop(0, first, lambda step, _: unused(block, step), None)
            lax.fori_loop(first, tiles, lambda step, _: used(block, step), None)

    def heads_of(ref, h, here):
        return jnp.concatenate([ref[here, lanes_of((first_head + h) * group + g)] for g in range(group)], 0)

    def tile_step(h, n, begin, length, blocks):
        lo = aligned(n * tile)
        here = pl.ds(lo, tile)
        query = heads_of(q_hat, h, here)
        grad_out = heads_of(do_ref, h, here)
        query_pos = base + lo + lax.broadcasted_iota(jnp.int32, (1, tile), 1)
        lower = first_visible(query_pos, jnp.zeros_like(query_pos)) - (origin + begin)
        lower = jnp.concatenate([lower] * group, 1)
        upper = jnp.concatenate([query_pos - (origin + begin)] * group, 1)
        offset = lax.broadcasted_iota(jnp.int32, (STRIP, lanes), 0)
        whole = isinstance(blocks, int)

        def fold(values):
            return values.reshape(STRIP // 8, 8, lanes)

        def over_blocks(step, init):
            return step(0, init) if whole else lax.fori_loop(0, blocks, step, init)

        def place_of(i):
            return 0 if whole else aligned(i * length)

        def strip(first, at):
            return pl.ds(first + at, STRIP)

        def products(i, top):
            first = place_of(i)
            keys = pl.ds(aligned(begin + first), length)
            score_buf[pl.ds(first, length)] = dot(k_hat[h, keys], query, (1, 1))
            soft_grad_buf[pl.ds(first, length)] = dot(v_buf[h, keys], grad_out, (1, 1))
            for at in range(0, length, STRIP):
                visible = offset >= lower - (first + at)
                if not whole or at + STRIP > length - tile:
                    visible &= offset <= upper - (first + at)
                sel = strip(first, at)
                part = jnp.where(visible, score_buf[sel], masked_score)
                score_buf[sel] = part
                top = jnp.maximum(top, jnp.max(fold(part), axis=0))
            return top

        top = over_blocks(products, jnp.full((8, lanes), masked_score, jnp.float32))
        top = jnp.max(top, axis=0, keepdims=True) * exp_scale

        def weigh(i, sums):
            first = place_of(i)
            total, product = sums
            for at in range(0, length, STRIP):
                sel = strip(first, at)
                weight = jnp.exp2(score_buf[sel] * exp_scale - top)
                score_buf[sel] = weight
                total += jnp.sum(fold(weight), axis=0)
                product += jnp.sum(fold(weight * soft_grad_buf[sel]), axis=0)
            return total, product

        total, product = over_blocks(weigh, (jnp.zeros((8, lanes), jnp.float32),) * 2)
        recip = 1.0 / jnp.sum(total, axis=0, keepdims=True)
        delta = jnp.sum(product, axis=0, keepdims=True) * recip
        out = pl.ds(aligned(n * lanes), lanes)

        def finish(i, _):
            first = place_of(i)
            keys = pl.ds(aligned(begin + first), length)
            for at in range(0, length, STRIP):
                sel = strip(first, at)
                soft = score_buf[sel] * recip
                soft_buf[at : at + STRIP] = soft.astype(jnp.bfloat16)
                ds_buf[at : at + STRIP] = (soft * (soft_grad_buf[sel] - delta)).astype(jnp.bfloat16)
            dk_acc[h, keys] += dot(ds_buf[:length], query, (1, 0))
            dv_acc[h, keys] += dot(soft_buf[:length], grad_out, (1, 0))
            grad = dot(k_turned[h, :, keys], ds_buf[:length], (1, 0))
            if whole:
                dq_out[h, :, out] = grad
            else:
                dq_out[h, :, out] += grad
            return 0

        if not whole:
            dq_out[h, :, out] = jnp.zeros((head, lanes), jnp.float32)
        over_blocks(finish, 0)

    def query_tile(h, n):
        end = far_rows + (n + 1) * tile
        need = end - (first_visible(base + n * tile, 0) - origin)
        lengths = [k * TILE for k in (3, 4, 6) if k * TILE <= far_rows + tile]
        for shorter, length in zip([0] + lengths, lengths):
            body = functools.partial(tile_step, h, n, aligned(end - length), length, 1)
            pl.when((need > shorter) & (need <= length))(body)
        count = (need + tile - 1) // tile
        body = functools.partial(tile_step, h, n, aligned(end - count * tile), tile, count)
        pl.when(need > max([0] + lengths))(body)

    mine = slice(far_rows, all_keys)

    def head_step(h, _):
        own = lanes_of(first_head + h)
        k_hat[h, mine] = k_own[:, own]
        v_buf[h, mine] = v_all[:, own]
        k_turned[h, :, mine] = k_own_turned[own]
        lax.fori_loop(0, tiles, lambda n, _: query_tile(h, n), None)
        dk_out[:, lanes_of(h)] = dk_acc[h, mine]
        dv_out[:, lanes_of(h)] = dv_acc[h, mine]

    dk_acc[...] = jnp.zeros_like(dk_acc)
    dv_acc[...] = jnp.zeros_like(dv_acc)
    over_far_keys(key_forward, key_hidden)
    lax.fori_loop(0, count, head_step, None)
    over_far_keys(key_backward, key_unused)
    gain_out[0, 0:1, :] = jnp.zeros((1, head), jnp.float32)
    gain_out[0, 1:2, :] = jnp.sum(gain_acc[...], axis=0, keepdims=True)


def attention(meta, gains, cos, sin, q_hat, k_hat, k_turned, do, v, far, first_head, count, docs):
    rows = q_hat.shape[0]
    head = gains.shape[1]
    group = q_hat.shape[1] // k_hat.shape[1]
    reach = len(far)
    operands = [meta, gains, cos, sin, q_hat, k_hat, k_turned, do, v, *far]
    keys = (reach + 1) * rows
    lanes = group * 2 * TILE
    out_shape = [jax.ShapeDtypeStruct((count, head, group * rows), jnp.float32)]
    out_shape += [jax.ShapeDtypeStruct((rows, count * head), jnp.float32)] * 2
    out_shape += [jax.ShapeDtypeStruct((rows, 2 * count * head), jnp.bfloat16)] * reach
    out_shape += [jax.ShapeDtypeStruct((1, 2, head), jnp.float32)]
    in_vmem = pl.BlockSpec(memory_space=pltpu.VMEM)
    return pl.pallas_call(
        functools.partial(attention_kernel, reach, docs, first_head, count),
        in_specs=[pl.BlockSpec(memory_space=pltpu.SMEM)] + [in_vmem] * (len(operands) - 1),
        out_specs=[in_vmem] * len(out_shape),
        scratch_shapes=[pltpu.VMEM((keys, lanes), jnp.float32)] * 2
        + [pltpu.VMEM((6 * TILE, lanes), jnp.bfloat16)] * 2
        + [pltpu.VMEM((count, keys, head), jnp.bfloat16)] * 2
        + [pltpu.VMEM((count, head, keys), jnp.bfloat16)]
        + [pltpu.VMEM((count, keys, head), jnp.float32)] * 2
        + [pltpu.VMEM((8, head), jnp.float32)],
        out_shape=out_shape,
        compiler_params=pltpu.CompilerParams(vmem_limit_bytes=24 * 1024 * 1024),
        cost_estimate=pl.CostEstimate(flops=1, bytes_accessed=1, transcendentals=0),
    )(*operands)


def backward_kernel(chained, first_head, parts, *refs):
    refs = refs[1 if chained else 0 :]
    gains_ref, cos_ref, sin_ref, turned_ref, q_ref, k_ref, dq_parts, dk_parts = refs[:8]
    part_refs = refs[8 : 8 + parts]
    dq_out, k_grads, gain_out, dq_buf, gain_acc, sem = refs[8 + parts :]
    count = dq_parts.shape[0]
    rows = q_ref.shape[0]
    head = gains_ref.shape[1]
    half = head // 2
    group = q_ref.shape[1] // k_ref.shape[1]
    gain_acc[...] = jnp.zeros_like(gain_acc)

    def query_step(n, _):
        lo = aligned(n * TILE)
        here = pl.ds(lo, TILE)
        cos, sin = turned_ref[:half, here], turned_ref[half:, here]
        for batch in in_batches(range(count * group), 4):
            turned = []
            for i in batch:
                at = (n // 2) * (2 * group * TILE) + (i % group) * 2 * TILE + (n % 2) * TILE
                grad = dq_parts[i // group, :, pl.ds(aligned(at), TILE)] * score_scale
                low, high = grad[:half], grad[half:]
                turned.append(jnp.concatenate([low * cos + high * sin, high * cos - low * sin], 0))
            turned = [jnp.transpose(t) for t in turned]
            raws = [q_ref[here, columns(first_head * group + i, head)] for i in batch]
            grads, gain_part = norm_backward(turned, raws, gains_ref[0:1, :])
            gain_acc[0:8] += gain_part
            for i, grad in zip(batch, grads):
                dq_buf[here, columns(i, head)] = grad.astype(jnp.bfloat16)

    def key_step(n, _):
        here = pl.ds(aligned(n * TILE), TILE)
        cos, sin = cos_ref[here], sin_ref[here]
        for batch in in_batches(range(count), 4):
            grads = [dk_parts[here, columns(j, head)] * score_scale for j in batch]
            turned = [dk * cos - pltpu.roll(dk, half, 1) * sin for dk in grads]
            raws = [k_ref[here, columns(first_head + j, head)] for j in batch]
            grads, gain_part = norm_backward(turned, raws, gains_ref[1:2, :])
            gain_acc[8:16] += gain_part
            for j, grad in zip(batch, grads):
                k_grads[here, columns(j, head)] = grad

    lax.fori_loop(0, rows // TILE, query_step, None)
    mine = dq_out.at[:, first_head * group * head : (first_head + count) * group * head]
    copy = pltpu.make_async_copy(dq_buf, mine, sem)
    copy.start()
    lax.fori_loop(0, rows // TILE, key_step, None)
    sums = [jnp.sum(gain_acc[at : at + 8], axis=0, keepdims=True) for at in (0, 8)]
    total = jnp.concatenate(sums, 0) + sum(ref[0] for ref in part_refs)
    gain_out[...] = jnp.broadcast_to(total[None], gain_out.shape)
    copy.wait()


def backward(gains, cos, sin, turned, q, k, dqs, dks, parts, carried, first_head, copies):
    count, head = dqs.shape[:2]
    group = q.shape[1] // k.shape[1]
    in_vmem = pl.BlockSpec(memory_space=pltpu.VMEM)
    operands = [gains, cos, sin, turned, q, k, dqs, dks, *parts]
    in_specs = [in_vmem] * len(operands)
    aliases = {}
    if carried is not None:
        operands.insert(0, carried)
        in_specs.insert(0, pl.BlockSpec(memory_space=pl.ANY))
        aliases = {0: 0}
    return pl.pallas_call(
        functools.partial(backward_kernel, carried is not None, first_head, len(parts)),
        in_specs=in_specs,
        out_specs=[pl.BlockSpec(memory_space=pl.ANY), in_vmem, in_vmem],
        scratch_shapes=[
            pltpu.VMEM((q.shape[0], count * group * head), jnp.bfloat16),
            pltpu.VMEM((16, head), jnp.float32),
            pltpu.SemaphoreType.DMA,
        ],
        out_shape=[
            jax.ShapeDtypeStruct(q.shape, jnp.bfloat16),
            jax.ShapeDtypeStruct(dks.shape, jnp.float32),
            jax.ShapeDtypeStruct((copies, *gains.shape), jnp.float32),
        ],
        input_output_aliases=aliases,
        compiler_params=pltpu.CompilerParams(vmem_limit_bytes=16 * 1024 * 1024),
        cost_estimate=pl.CostEstimate(flops=1, bytes_accessed=1, transcendentals=0),
    )(*operands)


def join_kernel(reach, own_key, own_value, *refs):
    width = own_key.shape[1]
    key_out, value_out = refs[-2:]
    key, value = own_key[...], own_value[...]
    for back in refs[:reach]:
        block = back[...].astype(jnp.float32)
        key = key + block[:, :width]
        value = value + block[:, width:]
    key_out[...] = key.astype(jnp.bfloat16)
    value_out[...] = value.astype(jnp.bfloat16)


def join(own_key, own_value, back, carried, place, like, cost):
    rows, width = own_key.shape
    reach = len(back)
    steps = 4
    operands = [own_key, own_value, *back]
    in_specs = [pl.BlockSpec((rows // steps, width), lambda i: (i, 0))] * 2
    in_specs += [pl.BlockSpec((rows // steps, 2 * width), lambda i: (i, 0))] * reach
    aliases = {}
    if carried is not None:
        aliases = {len(operands): 0, len(operands) + 1: 1}
        operands += carried
        in_specs += [pl.BlockSpec(memory_space=pl.ANY)] * 2
    return pl.pallas_call(
        functools.partial(join_kernel, reach),
        grid=(steps,),
        in_specs=in_specs,
        out_specs=[pl.BlockSpec((rows // steps, width), lambda i: (i, place))] * 2,
        out_shape=[jax.ShapeDtypeStruct(like.shape, like.dtype)] * 2,
        input_output_aliases=aliases,
        compiler_params=pltpu.CompilerParams(vmem_limit_bytes=8 * 1024 * 1024),
        cost_estimate=pl.CostEstimate(flops=1, bytes_accessed=cost, transcendentals=0),
    )(*operands)


def shards(
    query_raw, key_before_norm, value_input, out_cotangent, query_gain, key_norm_gain, doc_starts, windows
):
    rows = query_raw.shape[0]
    head = query_gain.shape[0]
    key_heads = key_before_norm.shape[1] // head
    shard_count = lax.axis_size("seq")
    slab_shards = shard_count // SLABS
    slab_length = slab_shards * rows
    shift = slab_length // 2 // rows
    assert slab_shards * SLABS == shard_count and shift * rows * 2 == slab_length
    reach = min((WINDOW - 1) // rows + 1, slab_shards - 1)
    docs = doc_starts.shape[1]

    def links(distance):
        found = []
        for i in range(shard_count):
            if (i - shift) % slab_shards + distance < slab_shards:
                found.append((i, (i + distance) % shard_count))
        return found

    placed = (lax.axis_index("seq") - shift) % shard_count
    slab = placed // slab_shards
    base = (placed % slab_shards) * rows
    starts = lax.dynamic_index_in_dim(doc_starts, slab, 0, keepdims=False)
    window = lax.dynamic_index_in_dim(windows, slab, 0, keepdims=True)
    meta = jnp.concatenate([base[None], window, starts]).astype(jnp.int32)
    positions = jnp.concatenate(
        [base - d * rows + jnp.arange(rows, dtype=jnp.int32) for d in range(reach + 1)]
    )
    begins = jnp.max(jnp.where(starts[None, :] <= positions[:, None], starts[None, :], 0), axis=1)
    spacing = jnp.arange(head // 2, dtype=jnp.float32) * (2.0 / head)
    angle = (positions - begins).astype(jnp.float32)[:, None] * (10000.0 ** (-spacing))[None, :]
    cosine, sine = jnp.cos(angle), jnp.sin(angle)
    count = 2 if key_heads % 2 == 0 else 1
    groups = range(0, key_heads, count)
    far = []
    sent = (key_before_norm, value_input)
    for j in groups:
        packed = jnp.concatenate([a[:, j * head : (j + count) * head] for a in sent], 1)
        far.append([lax.ppermute(packed, "seq", links(d)) for d in range(1, reach + 1)])
        if j == 0:
            *sent, cosine, sine = lax.optimization_barrier((*sent, cosine, sine))
    cos_table = jnp.concatenate([cosine, cosine], axis=1)
    sin_table = jnp.concatenate([-sine, sine], axis=1)
    across = (10000.0 ** (-spacing))[:, None] * (positions - begins)[:rows].astype(jnp.float32)[None, :]
    turned = jnp.concatenate([jnp.cos(across), jnp.sin(across)], axis=0)
    gains = jnp.stack([query_gain, key_norm_gain])

    q_hat, k_hat, k_turned = prepare(gains, cos_table, sin_table, query_raw, key_before_norm)
    query_gradient, everyone = None, None
    owns, backs = [], []
    for j, blocks in zip(groups, far):
        dqs, dks, value_own, *back, part = attention(
            meta, gains, cos_table, sin_table, q_hat, k_hat, k_turned, out_cotangent, value_input, blocks, j, count, docs
        )
        backs.append([lax.ppermute(b, "seq", [(to, at) for at, to in links(d)]) for d, b in enumerate(back, 1)])
        last = j + count == key_heads
        query_gradient, key_own, everyone = backward(
            gains, cos_table, sin_table, turned, query_raw, key_before_norm, dqs, dks,
            [part] if everyone is None else [part, everyone], query_gradient, j,
            lax.axis_size("head") if last else 1,
        )
        owns.append((key_own, value_own))
        if not last:
            meta, everyone = lax.optimization_barrier((meta, everyone))
    if len(backs) > 1:
        everyone, backs[:-1] = lax.optimization_barrier((everyone, backs[:-1]))
    near = jnp.sum(lax.all_to_all(everyone, "head", 0, 0), axis=0)
    gathered = lax.all_to_all(jnp.broadcast_to(near, (shard_count, *near.shape)), "seq", 0, 0)
    carried = None
    for n, (own, back) in enumerate(zip(owns, backs)):
        carried = join(*own, back, carried, n, key_before_norm, 1 if n + 1 < len(owns) else 200 * 10**6)
    total = jnp.sum(gathered, axis=0)
    return query_gradient, *carried, total[0], total[1]


def solution(mesh):
    placed = (P("seq", "head"),) * 4 + (P(),) * 4
    return jax.shard_map(
        shards,
        mesh=mesh,
        in_specs=placed,
        out_specs=(P("seq", "head"), P("seq", "head"), P("seq", "head"), P(), P()),
        check_vma=False,
    )
```

```python
import functools

import jax
import jax.numpy as jnp
from jax import lax
from jax.experimental import pallas as pl
from jax.experimental.pallas import tpu as pltpu
from jax.sharding import PartitionSpec as P

WINDOW = 1024
SLABS = 4

score_scale = 168.0 ** (-0.5)
log2_e = 1.4426950408889634
norm_eps = 1e-06
masked_score = -1e30
exp_scale = score_scale * log2_e

TILE = 128
STRIP = 32


def dot(a, b, contract):
    return lax.dot_general(a, b, ((contract[:1], contract[1:]), ((), ())), preferred_element_type=jnp.float32)


def inverse_rms(floats):
    return lax.rsqrt(jnp.mean(floats * floats, axis=-1, keepdims=True) + norm_eps)


def norm_forward(raws, gain, cosine, sine):
    floats = [raw.astype(jnp.float32) for raw in raws]
    inverses = [inverse_rms(f) for f in floats]
    scaled = [f * i * gain for f, i in zip(floats, inverses)]
    rolled = [pltpu.roll(s, s.shape[1] // 2, 1) for s in scaled]
    return [(s * cosine + r * sine).astype(jnp.bfloat16) for s, r in zip(scaled, rolled)]


def norm_backward(turned, raws, gain):
    floats = [raw.astype(jnp.float32) for raw in raws]
    inverses = [inverse_rms(f) for f in floats]
    weighted = [t * gain for t in turned]
    corrections = [jnp.mean(w * f, axis=-1, keepdims=True) for w, f in zip(weighted, floats)]
    gain_grad = sum(
        jnp.sum((t * (f * i)).reshape(-1, 8, t.shape[1]), axis=0) for t, f, i in zip(turned, floats, inverses)
    )
    grads = [
        i * w - f * (i * i * i * c) for f, i, w, c in zip(floats, inverses, weighted, corrections)
    ]
    return grads, gain_grad


def aligned(value):
    return pl.multiple_of(value, TILE)


def in_batches(items, size):
    return [items[n : n + size] for n in range(0, len(items), size)]


def columns(j, head):
    return slice(j * head, (j + 1) * head)


def prepare_kernel(gains_ref, cos_ref, sin_ref, q_ref, k_ref, q_hat, k_hat, k_turned):
    rows = q_ref.shape[0]
    head = gains_ref.shape[1]

    def step(n, _):
        here = pl.ds(aligned(n * TILE), TILE)
        cos, sin = cos_ref[here], sin_ref[here]
        for raw, row, out in ((q_ref, 0, q_hat), (k_ref, 1, k_hat)):
            for batch in in_batches(range(raw.shape[1] // head), 4):
                hats = norm_forward([raw[here, columns(j, head)] for j in batch], gains_ref[row : row + 1], cos, sin)
                for j, hat in zip(batch, hats):
                    out[here, columns(j, head)] = hat
                    if row == 1:
                        k_turned[columns(j, head), here] = jnp.transpose(hat)

    lax.fori_loop(0, rows // TILE, step, None)


def prepare(gains, cos, sin, q, k):
    in_vmem = pl.BlockSpec(memory_space=pltpu.VMEM)
    return pl.pallas_call(
        prepare_kernel,
        in_specs=[in_vmem] * 5,
        out_specs=[in_vmem] * 3,
        out_shape=[jax.ShapeDtypeStruct(shape, jnp.bfloat16) for shape in (q.shape, k.shape, k.shape[::-1])],
        compiler_params=pltpu.CompilerParams(vmem_limit_bytes=16 * 1024 * 1024),
        cost_estimate=pl.CostEstimate(flops=1, bytes_accessed=1, transcendentals=0),
    )(gains, cos, sin, q, k)


def attention_kernel(reach, docs, first_head, count, meta, *refs):
    gains_ref, cos_ref, sin_ref, q_hat, k_own, k_own_turned, do_ref, v_all = refs[:8]
    far_refs = refs[8 : 8 + reach]
    refs = refs[8 + reach :]
    dq_out, dk_out, dv_out = refs[:3]
    back_refs = refs[3 : 3 + reach]
    gain_out = refs[3 + reach]
    score_buf, soft_grad_buf, soft_buf, ds_buf, k_hat, v_buf, k_turned, dk_acc, dv_acc, gain_acc = refs[4 + reach :]
    rows = q_hat.shape[0]
    head = gains_ref.shape[1]
    half = head // 2
    group = q_hat.shape[1] // k_own.shape[1]
    tile = 2 * TILE
    lanes = group * tile
    tiles = rows // tile
    far_rows = reach * rows
    all_keys = far_rows + rows
    base, window = meta[0], meta[1]
    origin = base - far_rows
    k_gain = gains_ref[1:2, :]
    gain_acc[...] = jnp.zeros_like(gain_acc)

    def first_visible(position, zero):
        first = zero
        for j in range(docs):
            start = meta[2 + j]
            first = jnp.maximum(first, jnp.where(position >= start, start, 0))
        return jnp.maximum(first, position - window + 1)

    start_row = first_visible(base, 0) - origin

    def lanes_of(j):
        return pl.ds(aligned(j * head), head)

    def source(block, lo):
        far = far_refs[reach - block - 1]
        at = pl.ds(lo, tile)
        table = pl.ds(aligned((reach - block) * rows + lo), tile)
        raws = [far[at, columns(h, head)] for h in range(count)]
        values = [far[at, columns(count + h, head)] for h in range(count)]
        return raws, values, cos_ref[table], sin_ref[table]

    def key_forward(block, step):
        lo = aligned(step * tile)
        to = pl.ds(aligned(block * rows + lo), tile)
        raws, values, cos, sin = source(block, lo)
        hats = norm_forward(raws, k_gain, cos, sin)
        for h, (hat, value) in enumerate(zip(hats, values)):
            v_buf[h, to] = value
            k_hat[h, to] = hat
            k_turned[h, :, to] = jnp.transpose(hat)

    def key_hidden(block, step):
        to = pl.ds(aligned(block * rows + step * tile), tile)
        zeros = jnp.zeros((tile, head), jnp.bfloat16)
        for h in range(count):
            v_buf[h, to] = zeros
            k_hat[h, to] = zeros
            k_turned[h, :, to] = jnp.zeros((head, tile), jnp.bfloat16)

    def key_backward(block, step):
        lo = aligned(step * tile)
        sel = pl.ds(aligned(block * rows + lo), tile)
        raws, _, cos, sin = source(block, lo)
        grads = [dk_acc[h, sel] * score_scale for h in range(count)]
        turned = [dk * cos - pltpu.roll(dk, half, 1) * sin for dk in grads]
        grads, gain_part = norm_backward(turned, raws, k_gain)
        gain_acc[...] += gain_part
        back = back_refs[reach - block - 1]
        for h, grad in enumerate(grads):
            back[pl.ds(lo, tile), columns(h, head)] = grad.astype(jnp.bfloat16)
            back[pl.ds(lo, tile), columns(count + h, head)] = dv_acc[h, sel].astype(jnp.bfloat16)

    def key_unused(block, step):
        lo = aligned(step * tile)
        back_refs[reach - block - 1][pl.ds(lo, tile)] = jnp.zeros((tile, 2 * count * head), jnp.bfloat16)

    def over_far_keys(used, unused):
        for block in range(reach):
            first = jnp.clip((start_row - block * rows) // tile, 0, tiles)
            lax.fori_loop(0, first, lambda step, _: unused(block, step), None)
            lax.fori_loop(first, tiles, lambda step, _: used(block, step), None)

    def heads_of(ref, h, here):
        return jnp.concatenate([ref[here, lanes_of((first_head + h) * group + g)] for g in range(group)], 0)

    def tile_step(h, n, begin, length, blocks):
        lo = aligned(n * tile)
        here = pl.ds(lo, tile)
        query = heads_of(q_hat, h, here)
        grad_out = heads_of(do_ref, h, here)
        query_pos = base + lo + lax.broadcasted_iota(jnp.int32, (1, tile), 1)
        lower = first_visible(query_pos, jnp.zeros_like(query_pos)) - (origin + begin)
        lower = jnp.concatenate([lower] * group, 1)
        upper = jnp.concatenate([query_pos - (origin + begin)] * group, 1)
        offset = lax.broadcasted_iota(jnp.int32, (STRIP, lanes), 0)
        whole = isinstance(blocks, int)

        def fold(values):
            return values.reshape(STRIP // 8, 8, lanes)

        def over_blocks(step, init):
            return step(0, init) if whole else lax.fori_loop(0, blocks, step, init)

        def place_of(i):
            return 0 if whole else aligned(i * length)

        def strip(first, at):
            return pl.ds(first + at, STRIP)

        def products(i, top):
            first = place_of(i)
            keys = pl.ds(aligned(begin + first), length)
            score_buf[pl.ds(first, length)] = dot(k_hat[h, keys], query, (1, 1))
            soft_grad_buf[pl.ds(first, length)] = dot(v_buf[h, keys], grad_out, (1, 1))
            for at in range(0, length, STRIP):
                visible = offset >= lower - (first + at)
                if not whole or at + STRIP > length - tile:
                    visible &= offset <= upper - (first + at)
                sel = strip(first, at)
                part = jnp.where(visible, score_buf[sel], masked_score)
                score_buf[sel] = part
                top = jnp.maximum(top, jnp.max(fold(part), axis=0))
            return top

        top = over_blocks(products, jnp.full((8, lanes), masked_score, jnp.float32))
        top = jnp.max(top, axis=0, keepdims=True) * exp_scale

        def weigh(i, sums):
            first = place_of(i)
            total, product = sums
            for at in range(0, length, STRIP):
                sel = strip(first, at)
                weight = jnp.exp2(score_buf[sel] * exp_scale - top)
                score_buf[sel] = weight
                total += jnp.sum(fold(weight), axis=0)
                product += jnp.sum(fold(weight * soft_grad_buf[sel]), axis=0)
            return total, product

        total, product = over_blocks(weigh, (jnp.zeros((8, lanes), jnp.float32),) * 2)
        recip = 1.0 / jnp.sum(total, axis=0, keepdims=True)
        delta = jnp.sum(product, axis=0, keepdims=True) * recip
        out = pl.ds(aligned(n * lanes), lanes)

        def finish(i, _):
            first = place_of(i)
            keys = pl.ds(aligned(begin + first), length)
            for at in range(0, length, STRIP):
                sel = strip(first, at)
                soft = score_buf[sel] * recip
                soft_buf[at : at + STRIP] = soft.astype(jnp.bfloat16)
                ds_buf[at : at + STRIP] = (soft * (soft_grad_buf[sel] - delta)).astype(jnp.bfloat16)
            dk_acc[h, keys] += dot(ds_buf[:length], query, (1, 0))
            dv_acc[h, keys] += dot(soft_buf[:length], grad_out, (1, 0))
            grad = dot(k_turned[h, :, keys], ds_buf[:length], (1, 0))
            if whole:
                dq_out[h, :, out] = grad
            else:
                dq_out[h, :, out] += grad
            return 0

        if not whole:
            dq_out[h, :, out] = jnp.zeros((head, lanes), jnp.float32)
        over_blocks(finish, 0)

    def query_tile(h, n):
        end = far_rows + (n + 1) * tile
        need = end - (first_visible(base + n * tile, 0) - origin)
        lengths = [k * TILE for k in (3, 4, 6) if k * TILE <= far_rows + tile]
        for shorter, length in zip([0] + lengths, lengths):
            body = functools.partial(tile_step, h, n, aligned(end - length), length, 1)
            pl.when((need > shorter) & (need <= length))(body)
        count = (need + tile - 1) // tile
        body = functools.partial(tile_step, h, n, aligned(end - count * tile), tile, count)
        pl.when(need > max([0] + lengths))(body)

    mine = slice(far_rows, all_keys)

    def head_step(h, _):
        own = lanes_of(first_head + h)
        k_hat[h, mine] = k_own[:, own]
        v_buf[h, mine] = v_all[:, own]
        k_turned[h, :, mine] = k_own_turned[own]
        lax.fori_loop(0, tiles, lambda n, _: query_tile(h, n), None)
        dk_out[:, lanes_of(h)] = dk_acc[h, mine]
        dv_out[:, lanes_of(h)] = dv_acc[h, mine]

    dk_acc[...] = jnp.zeros_like(dk_acc)
    dv_acc[...] = jnp.zeros_like(dv_acc)
    over_far_keys(key_forward, key_hidden)
    lax.fori_loop(0, count, head_step, None)
    over_far_keys(key_backward, key_unused)
    gain_out[0, 0:1, :] = jnp.zeros((1, head), jnp.float32)
    gain_out[0, 1:2, :] = jnp.sum(gain_acc[...], axis=0, keepdims=True)


def attention(meta, gains, cos, sin, q_hat, k_hat, k_turned, do, v, far, first_head, count, docs):
    rows = q_hat.shape[0]
    head = gains.shape[1]
    group = q_hat.shape[1] // k_hat.shape[1]
    reach = len(far)
    operands = [meta, gains, cos, sin, q_hat, k_hat, k_turned, do, v, *far]
    keys = (reach + 1) * rows
    lanes = group * 2 * TILE
    out_shape = [jax.ShapeDtypeStruct((count, head, group * rows), jnp.float32)]
    out_shape += [jax.ShapeDtypeStruct((rows, count * head), jnp.float32)] * 2
    out_shape += [jax.ShapeDtypeStruct((rows, 2 * count * head), jnp.bfloat16)] * reach
    out_shape += [jax.ShapeDtypeStruct((1, 2, head), jnp.float32)]
    in_vmem = pl.BlockSpec(memory_space=pltpu.VMEM)
    return pl.pallas_call(
        functools.partial(attention_kernel, reach, docs, first_head, count),
        in_specs=[pl.BlockSpec(memory_space=pltpu.SMEM)] + [in_vmem] * (len(operands) - 1),
        out_specs=[in_vmem] * len(out_shape),
        scratch_shapes=[pltpu.VMEM((keys, lanes), jnp.float32)] * 2
        + [pltpu.VMEM((6 * TILE, lanes), jnp.bfloat16)] * 2
        + [pltpu.VMEM((count, keys, head), jnp.bfloat16)] * 2
        + [pltpu.VMEM((count, head, keys), jnp.bfloat16)]
        + [pltpu.VMEM((count, keys, head), jnp.float32)] * 2
        + [pltpu.VMEM((8, head), jnp.float32)],
        out_shape=out_shape,
        compiler_params=pltpu.CompilerParams(vmem_limit_bytes=24 * 1024 * 1024),
        cost_estimate=pl.CostEstimate(flops=1, bytes_accessed=1, transcendentals=0),
    )(*operands)


def backward_kernel(chained, first_head, parts, *refs):
    refs = refs[1 if chained else 0 :]
    gains_ref, cos_ref, sin_ref, turned_ref, q_ref, k_ref, dq_parts, dk_parts = refs[:8]
    part_refs = refs[8 : 8 + parts]
    dq_out, k_grads, gain_out, dq_buf, gain_acc, sem = refs[8 + parts :]
    count = dq_parts.shape[0]
    rows = q_ref.shape[0]
    head = gains_ref.shape[1]
    half = head // 2
    group = q_ref.shape[1] // k_ref.shape[1]
    gain_acc[...] = jnp.zeros_like(gain_acc)

    def query_step(n, _):
        lo = aligned(n * TILE)
        here = pl.ds(lo, TILE)
        cos, sin = turned_ref[:half, here], turned_ref[half:, here]
        for batch in in_batches(range(count * group), 4):
            turned = []
            for i in batch:
                at = (n // 2) * (2 * group * TILE) + (i % group) * 2 * TILE + (n % 2) * TILE
                grad = dq_parts[i // group, :, pl.ds(aligned(at), TILE)] * score_scale
                low, high = grad[:half], grad[half:]
                turned.append(jnp.concatenate([low * cos + high * sin, high * cos - low * sin], 0))
            turned = [jnp.transpose(t) for t in turned]
            raws = [q_ref[here, columns(first_head * group + i, head)] for i in batch]
            grads, gain_part = norm_backward(turned, raws, gains_ref[0:1, :])
            gain_acc[0:8] += gain_part
            for i, grad in zip(batch, grads):
                dq_buf[here, columns(i, head)] = grad.astype(jnp.bfloat16)

    def key_step(n, _):
        here = pl.ds(aligned(n * TILE), TILE)
        cos, sin = cos_ref[here], sin_ref[here]
        for batch in in_batches(range(count), 4):
            grads = [dk_parts[here, columns(j, head)] * score_scale for j in batch]
            turned = [dk * cos - pltpu.roll(dk, half, 1) * sin for dk in grads]
            raws = [k_ref[here, columns(first_head + j, head)] for j in batch]
            grads, gain_part = norm_backward(turned, raws, gains_ref[1:2, :])
            gain_acc[8:16] += gain_part
            for j, grad in zip(batch, grads):
                k_grads[here, columns(j, head)] = grad

    lax.fori_loop(0, rows // TILE, query_step, None)
    mine = dq_out.at[:, first_head * group * head : (first_head + count) * group * head]
    copy = pltpu.make_async_copy(dq_buf, mine, sem)
    copy.start()
    lax.fori_loop(0, rows // TILE, key_step, None)
    sums = [jnp.sum(gain_acc[at : at + 8], axis=0, keepdims=True) for at in (0, 8)]
    total = jnp.concatenate(sums, 0) + sum(ref[0] for ref in part_refs)
    gain_out[...] = jnp.broadcast_to(total[None], gain_out.shape)
    copy.wait()


def backward(gains, cos, sin, turned, q, k, dqs, dks, parts, carried, first_head, copies):
    count, head = dqs.shape[:2]
    group = q.shape[1] // k.shape[1]
    in_vmem = pl.BlockSpec(memory_space=pltpu.VMEM)
    operands = [gains, cos, sin, turned, q, k, dqs, dks, *parts]
    in_specs = [in_vmem] * len(operands)
    aliases = {}
    if carried is not None:
        operands.insert(0, carried)
        in_specs.insert(0, pl.BlockSpec(memory_space=pl.ANY))
        aliases = {0: 0}
    return pl.pallas_call(
        functools.partial(backward_kernel, carried is not None, first_head, len(parts)),
        in_specs=in_specs,
        out_specs=[pl.BlockSpec(memory_space=pl.ANY), in_vmem, in_vmem],
        scratch_shapes=[
            pltpu.VMEM((q.shape[0], count * group * head), jnp.bfloat16),
            pltpu.VMEM((16, head), jnp.float32),
            pltpu.SemaphoreType.DMA,
        ],
        out_shape=[
            jax.ShapeDtypeStruct(q.shape, jnp.bfloat16),
            jax.ShapeDtypeStruct(dks.shape, jnp.float32),
            jax.ShapeDtypeStruct((copies, *gains.shape), jnp.float32),
        ],
        input_output_aliases=aliases,
        compiler_params=pltpu.CompilerParams(vmem_limit_bytes=16 * 1024 * 1024),
        cost_estimate=pl.CostEstimate(flops=1, bytes_accessed=1, transcendentals=0),
    )(*operands)


def join_kernel(reach, own_key, own_value, *refs):
    width = own_key.shape[1]
    key_out, value_out = refs[-2:]
    key, value = own_key[...], own_value[...]
    for back in refs[:reach]:
        block = back[...].astype(jnp.float32)
        key = key + block[:, :width]
        value = value + block[:, width:]
    key_out[...] = key.astype(jnp.bfloat16)
    value_out[...] = value.astype(jnp.bfloat16)


def join(own_key, own_value, back, carried, place, like, cost):
    rows, width = own_key.shape
    reach = len(back)
    steps = 4
    operands = [own_key, own_value, *back]
    in_specs = [pl.BlockSpec((rows // steps, width), lambda i: (i, 0))] * 2
    in_specs += [pl.BlockSpec((rows // steps, 2 * width), lambda i: (i, 0))] * reach
    aliases = {}
    if carried is not None:
        aliases = {len(operands): 0, len(operands) + 1: 1}
        operands += carried
        in_specs += [pl.BlockSpec(memory_space=pl.ANY)] * 2
    return pl.pallas_call(
        functools.partial(join_kernel, reach),
        grid=(steps,),
        in_specs=in_specs,
        out_specs=[pl.BlockSpec((rows // steps, width), lambda i: (i, place))] * 2,
        out_shape=[jax.ShapeDtypeStruct(like.shape, like.dtype)] * 2,
        input_output_aliases=aliases,
        compiler_params=pltpu.CompilerParams(vmem_limit_bytes=8 * 1024 * 1024),
        cost_estimate=pl.CostEstimate(flops=1, bytes_accessed=cost, transcendentals=0),
    )(*operands)


def shards(
    query_raw, key_before_norm, value_input, out_cotangent, query_gain, key_norm_gain, doc_starts, windows
):
    rows = query_raw.shape[0]
    head = query_gain.shape[0]
    key_heads = key_before_norm.shape[1] // head
    shard_count = lax.axis_size("seq")
    slab_shards = shard_count // SLABS
    slab_length = slab_shards * rows
    shift = slab_length // 2 // rows
    assert slab_shards * SLABS == shard_count and shift * rows * 2 == slab_length
    reach = min((WINDOW - 1) // rows + 1, slab_shards - 1)
    docs = doc_starts.shape[1]

    def links(distance):
        found = []
        for i in range(shard_count):
            if (i - shift) % slab_shards + distance < slab_shards:
                found.append((i, (i + distance) % shard_count))
        return found

    placed = (lax.axis_index("seq") - shift) % shard_count
    slab = placed // slab_shards
    base = (placed % slab_shards) * rows
    starts = lax.dynamic_index_in_dim(doc_starts, slab, 0, keepdims=False)
    window = lax.dynamic_index_in_dim(windows, slab, 0, keepdims=True)
    meta = jnp.concatenate([base[None], window, starts]).astype(jnp.int32)
    positions = jnp.concatenate(
        [base - d * rows + jnp.arange(rows, dtype=jnp.int32) for d in range(reach + 1)]
    )
    begins = jnp.max(jnp.where(starts[None, :] <= positions[:, None], starts[None, :], 0), axis=1)
    spacing = jnp.arange(head // 2, dtype=jnp.float32) * (2.0 / head)
    angle = (positions - begins).astype(jnp.float32)[:, None] * (10000.0 ** (-spacing))[None, :]
    cosine, sine = jnp.cos(angle), jnp.sin(angle)
    cos_table = jnp.concatenate([cosine, cosine], axis=1)
    sin_table = jnp.concatenate([-sine, sine], axis=1)
    across = (10000.0 ** (-spacing))[:, None] * (positions - begins)[:rows].astype(jnp.float32)[None, :]
    turned = jnp.concatenate([jnp.cos(across), jnp.sin(across)], axis=0)
    gains = jnp.stack([query_gain, key_norm_gain])

    q_hat, k_hat, k_turned = prepare(gains, cos_table, sin_table, query_raw, key_before_norm)
    count = 2 if key_heads % 2 == 0 else 1
    groups = range(0, key_heads, count)
    far = []
    sent = (key_before_norm, value_input)
    for j in groups:
        packed = jnp.concatenate([a[:, j * head : (j + count) * head] for a in sent], 1)
        far.append([lax.ppermute(packed, "seq", links(d)) for d in range(1, reach + 1)])
        if j == 0:
            *sent, k_hat = lax.optimization_barrier((*sent, k_hat))
    query_gradient, everyone = None, None
    owns, backs = [], []
    for j, blocks in zip(groups, far):
        dqs, dks, value_own, *back, part = attention(
            meta, gains, cos_table, sin_table, q_hat, k_hat, k_turned, out_cotangent, value_input, blocks, j, count, docs
        )
        backs.append([lax.ppermute(b, "seq", [(to, at) for at, to in links(d)]) for d, b in enumerate(back, 1)])
        last = j + count == key_heads
        query_gradient, key_own, everyone = backward(
            gains, cos_table, sin_table, turned, query_raw, key_before_norm, dqs, dks,
            [part] if everyone is None else [part, everyone], query_gradient, j,
            shard_count * lax.axis_size("head") if last else 1,
        )
        owns.append((key_own, value_own))
        if not last:
            meta, everyone = lax.optimization_barrier((meta, everyone))
    if len(backs) > 1:
        everyone, backs[:-1] = lax.optimization_barrier((everyone, backs[:-1]))
    gathered = lax.all_to_all(everyone, ("seq", "head"), 0, 0)
    carried = None
    for n, (own, back) in enumerate(zip(owns, backs)):
        carried = join(*own, back, carried, n, key_before_norm, 1 if n + 1 < len(owns) else 200 * 10**6)
    total = jnp.sum(gathered, axis=0)
    return query_gradient, *carried, total[0], total[1]


def solution(mesh):
    placed = (P("seq", "head"),) * 4 + (P(),) * 4
    return jax.shard_map(
        shards,
        mesh=mesh,
        in_specs=placed,
        out_specs=(P("seq", "head"), P("seq", "head"), P("seq", "head"), P(), P()),
        check_vma=False,
    )
```
